512 devices in a mesh: rep: 8 (over x, core), row: 64 (over z, y).
Axes of the slice: x: 4, y: 8, z: 8, core: 2. Of those that a mesh axis runs over, the one named last changes fastest.
Arguments:
- weight: bfloat16 [8192, 384], P('row'), may hold values from -0.0625 to 0.0625
- first_moment: bfloat16 [8, 8192, 384], P('rep', 'row'), may hold values from -0.29882812 to 0.29882812
- second_moment: bfloat16 [8, 8192, 384], P('rep', 'row'), may hold values from 2.9921532e-05 to 0.0029907227
- token_ids: int32 [8, 4, 1024], P('rep'), may hold values from 0 to 1535
- shared_inputs: bfloat16 [1024, 8192], P(None, 'row'), may hold values from -6 to 6
- private_inputs: bfloat16 [8, 512, 8192], P('rep', None, 'row'), may hold values from -6 to 6
- shared_targets: bfloat16 [1024, 384], replicated, may hold values from -6 to 6
- private_targets: bfloat16 [8, 512, 384], P('rep'), may hold values from -6 to 6
Outputs:
- merged: float32 [8192, 384], P(('row', 'rep'))
The draws below stay inside these ranges and needn't reach their ends.
All inputs are finite; a program needn't handle non-finite values.
Results may differ from the reference program's by a relative error of at most 0.0005.
The reference program's roundings to bfloat16 on the way count: a program that leaves them out, or rounds other values in their place, can miss the bound.
Values sent between devices are 32-bit elements; how exact they have to be, the bound alone decides.
No kernel may reach another device: no remote copies, remote signals or barrier semaphores. Data moves between devices by JAX's collectives and lax.ppermute only.
A program may use at most 64 MiB of HBM per device.

```python
import math
import jax
import jax.numpy as jnp
from jax import lax

R = 8192
C = 384
TOK = 1024
POOL = 1024
PRIV = 512
STEPS = 4
REPLICAS = 8


def with_ends(array, own_key, least, largest):
    spot = [jax.random.randint(jax.random.fold_in(own_key, axis), (), 0, length) for axis, length in enumerate(array.shape)]
    main_axis = array.shape.index(max(array.shape))
    neighbour = spot[:main_axis] + [(spot[main_axis] + 1) % array.shape[main_axis]] + spot[main_axis + 1:]
    return array.at[tuple(spot)].set(least).at[tuple(neighbour)].set(largest)


def level_of(stream_key, extent, shards, low, largest):
    def one(dim, blocks):
        steps = jax.random.uniform(jax.random.fold_in(jax.random.fold_in(stream_key, 6), dim), (blocks,), jnp.float32, low / len(shards), largest / len(shards))
        return jnp.repeat(jnp.exp(steps), extent[dim] // blocks).reshape((-1,) + (1,) * (len(extent) - dim - 1))

    factor_of = one(*shards[0])
    for cut in shards[1:]:
        factor_of = factor_of * one(*cut)
    return factor_of


def centred(stream_key, dims, scale, limit, shards=(), dtype=jnp.bfloat16):
    entries = jax.random.normal(stream_key, dims, jnp.float32) * scale
    if len(shards) > 0:
        entries = level_of(stream_key, dims, shards, -0.22, 0.18) * entries
    return jnp.clip(entries, min=-limit, max=limit).astype(dtype)


def setup_inputs(seed: int = 0) -> dict:
    splits = jax.random.split(jax.random.key(seed), 9)
    weight = centred(splits[0], (R, C), R ** -0.5, 0.0625, ((0, 64),))
    first_moment = centred(splits[1], (REPLICAS, R, C), 0.05, 0.29882812, ((0, 8), (1, 64)))
    second_moment = jnp.clip(jnp.exp(math.log(0.0029907227) - 4.604692 * jax.random.uniform(splits[2], (REPLICAS, R, C), jnp.float32) ** level_of(splits[2], (REPLICAS, R, C), ((0, 8), (1, 64)), -0.2, 0.2)), 2.9921531677246094e-05, 0.0029907227).astype(jnp.bfloat16)
    token_ids = with_ends(jax.random.randint(splits[3], (REPLICAS, STEPS, TOK), 0, POOL + PRIV), jax.random.fold_in(splits[3], 1), 0, (POOL + PRIV) - 1).astype(jnp.int32)
    shared_inputs = centred(splits[4], (POOL, R), 1.0, 6.0, ((1, 64),))
    private_inputs = centred(splits[5], (REPLICAS, PRIV, R), 1.0, 6.0, ((0, 8), (2, 64)))
    shared_targets = centred(splits[6], (POOL, C), 1.0, 6.0)
    private_targets = centred(splits[7], (REPLICAS, PRIV, C), 1.0, 6.0, ((0, 8),))
    return dict(weight=weight, first_moment=first_moment, second_moment=second_moment, token_ids=token_ids, shared_inputs=shared_inputs, private_inputs=private_inputs, shared_targets=shared_targets, private_targets=private_targets)


learn_rate = 0.001
beta_one = 0.9
beta_two = 0.95
adam_eps = 1e-08
weight_decay = 0.1
norm_eps = 1e-06

def combine_pair(lower_vec, upper_vec, cross_dot, lower_norm, upper_norm):
    lower_coef = 1.0 - cross_dot / (2.0 * (lower_norm + norm_eps))
    upper_coef = 1.0 - cross_dot / (2.0 * (upper_norm + norm_eps))
    return lower_coef * lower_vec + upper_coef * upper_vec

def reference(weight, first_moment, second_moment, token_ids, shared_inputs, private_inputs, shared_targets, private_targets):
    weight_start = weight.astype(jnp.float32)

    def replica_run(items):
        moment_one, moment_two, replica_ids, own_inputs, own_targets = items
        input_table = jnp.concatenate([shared_inputs, own_inputs], axis=0)
        target_table = jnp.concatenate([shared_targets, own_targets], axis=0)
        moment_one = moment_one.astype(jnp.float32)
        moment_two = moment_two.astype(jnp.float32)
        update_sum = jnp.zeros(weight_start.shape, jnp.float32)
        for step_index in range(STEPS):
            tok_rows = jnp.take(input_table, replica_ids[step_index], axis=0)
            targets = jnp.take(target_table, replica_ids[step_index], axis=0)
            weight_now = weight_start - learn_rate * update_sum
            weight_bf = weight_now.astype(jnp.bfloat16)
            output = jnp.dot(tok_rows, weight_bf, preferred_element_type=jnp.float32)
            residual = (output - targets.astype(jnp.float32)).astype(jnp.bfloat16)
            gradient = jnp.dot(tok_rows.T, residual, preferred_element_type=jnp.float32) / TOK
            moment_one = beta_one * moment_one + (1.0 - beta_one) * gradient
            moment_two = beta_two * moment_two + (1.0 - beta_two) * gradient * gradient
            direction = moment_one / (jnp.sqrt(moment_two) + adam_eps) + weight_decay * weight_now
            update_sum = update_sum + direction
        return update_sum
    deltas = lax.map(replica_run, (first_moment, second_moment, token_ids, private_inputs, private_targets))
    current = deltas
    while current.shape[0] > 1:
        paired = current.reshape(current.shape[0] // 2, 2, current.shape[1], current.shape[2])
        lower_vec = paired[:, 0]
        upper_vec = paired[:, 1]
        cross_dot = lax.optimization_barrier(jnp.sum(lower_vec * upper_vec, axis=(1, 2)))[:, None, None]
        lower_norm = lax.optimization_barrier(jnp.sum(lower_vec * lower_vec, axis=(1, 2)))[:, None, None]
        upper_norm = lax.optimization_barrier(jnp.sum(upper_vec * upper_vec, axis=(1, 2)))[:, None, None]
        current = combine_pair(lower_vec, upper_vec, cross_dot, lower_norm, upper_norm)
    return current[0]
```

```python
import functools

import jax
import jax.numpy as jnp
from jax import lax
from jax.experimental import pallas as pl
from jax.experimental.pallas import tpu as pltpu
from jax.sharding import Mesh
from jax.sharding import PartitionSpec as P

CZY = ("core", "z", "y")
F32 = jnp.float32
BF16 = jnp.bfloat16

learn_rate = 0.001
beta_one = 0.9
beta_two = 0.95
adam_eps = 1e-08
weight_decay = 0.1
norm_eps = 1e-06

SIDE = 8
LANES = 128
COLS = 48
HALF = COLS // 2
TILE = COLS + HALF
POOL = 1024
TABLE = 1536
STEPS = 4
TOKENS = 1024
REPLICAS = 8
PAIRS = [(i, j) for i in range(REPLICAS) for j in range(i, REPLICAS)]
VMEM = 48 * 1024 * 1024


def position(core, z, y):
    return (core * SIDE + z) * SIDE + y


SUM_GROUPS = [[position(0, z, y) for z in range(SIDE)] for y in range(SIDE)] + [
    [position(1, z, y) for y in range(SIDE)] for z in range(SIDE)
]
GATHER_GROUPS = [[position(0, z, y) for y in range(SIDE)] for z in range(SIDE)] + [
    [position(1, z, y) for z in range(SIDE)] for y in range(SIDE)
]


def exchange(blocks, axes, groups=None):
    return lax.all_to_all(
        blocks, axes, split_axis=0, concat_axis=0, tiled=True, axis_index_groups=groups
    )


def kernel_call(body, out_shapes, *operands):
    return pl.pallas_call(
        body,
        out_shape=out_shapes,
        compiler_params=pltpu.CompilerParams(vmem_limit_bytes=VMEM),
    )(*operands)


def shaped(*dims, dtype=F32):
    return jax.ShapeDtypeStruct(dims, dtype)


def store_output(out_ref, output):
    for j in range(SIDE):
        out_ref[j, :COLS, :] = output[:, j * LANES : (j + 1) * LANES]
        private = POOL + (j // 2) * LANES
        line = (j % 2) * HALF
        out_ref[j, COLS:, :] = output[line : line + HALF, private : private + LANES]


def states_kernel(w_ref, m_ref, v_ref, out_ref):
    for part, ref in enumerate((w_ref, m_ref, v_ref)):
        turned = ref[...].astype(F32).T.reshape(SIDE, COLS, LANES)
        out_ref[:, part * COLS : (part + 1) * COLS, :] = turned


def first_kernel(x_ref, w_ref, table_ref, out_ref, total):
    step = pl.program_id(0)
    block = jnp.concatenate([x_ref[0], x_ref[1]], axis=1).astype(BF16)
    table_ref[...] = block
    weights = jnp.concatenate([w_ref[0], w_ref[1]], axis=1).astype(BF16)
    part = lax.dot_general(
        weights, block, (((1,), (1,)), ((), ())), preferred_element_type=F32
    )

    @pl.when(step == 0)
    def _():
        total[...] = part

    @pl.when(step > 0)
    def _():
        total[...] += part

    @pl.when(step == pl.num_programs(0) - 1)
    def _():
        store_output(out_ref, total[...])


def first_output(gathered, states):
    return pl.pallas_call(
        first_kernel,
        grid=(SIDE // 2,),
        in_specs=[
            pl.BlockSpec((2, TABLE, LANES), lambda i: (i, 0, 0)),
            pl.BlockSpec((2, COLS, LANES), lambda i: (i, 0, 0)),
        ],
        out_specs=[
            pl.BlockSpec((TABLE, 2 * LANES), lambda i: (0, i)),
            pl.BlockSpec((SIDE, TILE, LANES), lambda i: (0, 0, 0)),
        ],
        out_shape=[shaped(TABLE, SIDE * LANES, dtype=BF16), shaped(SIDE, TILE, LANES)],
        scratch_shapes=[pltpu.VMEM((COLS, TABLE), F32)],
        compiler_params=pltpu.CompilerParams(vmem_limit_bytes=VMEM),
    )(gathered, states)


def error_kernel(step, parts_ref, target_ref, count_ref, out_ref):
    output = parts_ref[0]
    for j in range(1, SIDE):
        output = output + parts_ref[j]
    error = (output - target_ref[...]).astype(BF16).astype(F32)
    weighted = error * count_ref[step]
    for j in range(SIDE):
        out_ref[j] = weighted


def step_kernel(first, last, error_ref, table_ref, w_ref, states_ref, *rest):
    if last:
        (total_out,) = rest
        new_states = None
    else:
        new_states, output_ref = rest
    error = jnp.concatenate(
        [error_ref[j, :COLS, :] for j in range(SIDE)]
        + [
            jnp.concatenate([error_ref[2 * k, COLS:, :], error_ref[2 * k + 1, COLS:, :]], axis=0)
            for k in range(SIDE // 2)
        ],
        axis=1,
    )
    high = error.astype(BF16)
    low = (error - high.astype(F32)).astype(BF16)
    both = jnp.concatenate([high, low], axis=0)
    wide = 2 * LANES
    updated = []
    for k in range(SIDE // 2):
        product = jnp.dot(both, table_ref[:, k * wide : (k + 1) * wide], preferred_element_type=F32)
        gradients = (product[:COLS] + product[COLS:]) * (1.0 / TOKENS)
        for half in range(2):
            j = 2 * k + half
            gradient = gradients[:, half * LANES : (half + 1) * LANES]
            weight_start = w_ref[j, :COLS, :]
            if first:
                weight_now = weight_start
            else:
                update_sum = states_ref[j, 2 * COLS :, :]
                weight_now = weight_start - learn_rate * update_sum
            base = COLS if first else 0
            moment_one = states_ref[j, base : base + COLS, :]
            moment_two = states_ref[j, base + COLS : base + 2 * COLS, :]
            moment_one = beta_one * moment_one + (1.0 - beta_one) * gradient
            moment_two = beta_two * moment_two + (1.0 - beta_two) * gradient * gradient
            direction = (
                moment_one / (jnp.sqrt(moment_two) + adam_eps) + weight_decay * weight_now
            )
            update_sum = direction if first else update_sum + direction
            if last:
                total_out[j] = update_sum
            else:
                new_states[j, :COLS, :] = moment_one
                new_states[j, COLS : 2 * COLS, :] = moment_two
                new_states[j, 2 * COLS :, :] = update_sum
                updated.append((weight_start - learn_rate * update_sum).astype(BF16))
    if last:
        return
    weights = jnp.concatenate(updated, axis=1)
    output = jnp.concatenate(
        [
            lax.dot_general(
                weights,
                table_ref[row : row + wide, :],
                (((1,), (1,)), ((), ())),
                preferred_element_type=F32,
            )
            for row in range(0, TABLE, wide)
        ],
        axis=1,
    )
    store_output(output_ref, output)


def turn_kernel(parts_ref, out_ref):
    turned = parts_ref[...].reshape(SIDE * COLS, LANES).T
    out_ref[...] = turned.reshape(REPLICAS, LANES // REPLICAS, SIDE * COLS)


def gram_kernel(updates_ref, out_ref):
    updates = [updates_ref[r] for r in range(REPLICAS)]
    lines = []
    for i, j in PAIRS:
        product = updates[i] * updates[j]
        lines.append(jnp.sum(product, axis=0, keepdims=True))
    while len(lines) % 8:
        lines.append(jnp.zeros_like(lines[0]))
    sums = jnp.sum(jnp.concatenate(lines, axis=0), axis=1, keepdims=True)
    spread = jnp.broadcast_to(sums, (len(lines), LANES))
    line = lax.broadcasted_iota(jnp.int32, spread.shape, 0)
    lane = lax.broadcasted_iota(jnp.int32, spread.shape, 1)
    packed = jnp.sum(jnp.where(line == lane, spread, 0.0), axis=0, keepdims=True)
    for j in range(REPLICAS):
        out_ref[j] = packed


def gram_sum_kernel(parts_ref, out_ref):
    packed = jnp.sum(parts_ref[...], axis=0)
    for j in range(SIDE * SIDE):
        out_ref[j] = packed


def merge_kernel(parts_ref, updates_ref, out_ref):
    packed = jnp.sum(parts_ref[...], axis=0)
    lane = lax.broadcasted_iota(jnp.int32, packed.shape, 1)
    gram = {}
    for place, (i, j) in enumerate(PAIRS):
        value = jnp.sum(jnp.where(lane == place, packed, 0.0), axis=1, keepdims=True)
        gram[i, j] = value
        gram[j, i] = value
    members = [[r] for r in range(REPLICAS)]
    while len(members) > 1:
        merged = []
        for lower, upper in zip(members[0::2], members[1::2]):
            cross_dot = sum(gram[i, j] for i in lower for j in upper)
            lower_norm = sum(gram[i, j] for i in lower for j in lower)
            upper_norm = sum(gram[i, j] for i in upper for j in upper)
            lower_coef = 1.0 - cross_dot / (2.0 * (lower_norm + norm_eps))
            upper_coef = 1.0 - cross_dot / (2.0 * (upper_norm + norm_eps))
            scale = {**{i: lower_coef for i in lower}, **{i: upper_coef for i in upper}}
            merged.append((lower + upper, scale))
        factor = {i: scale[i] for _, scale in merged for i in scale}
        gram = {(i, j): factor[i] * factor[j] * value for (i, j), value in gram.items()}
        total = factor if len(merged) * 2 == REPLICAS else {i: total[i] * factor[i] for i in total}
        members = [group for group, _ in merged]
    result = total[0] * updates_ref[0]
    for r in range(1, REPLICAS):
        result = result + total[r] * updates_ref[r]
    out_ref[...] = result


def own_targets(shared_targets, private_targets, sum_place, gather_place):
    rows = lax.dynamic_slice_in_dim(shared_targets, sum_place * LANES, LANES, 0)
    shared = lax.dynamic_slice_in_dim(rows.astype(F32).T, gather_place * COLS, COLS, 0)
    rows = lax.dynamic_slice_in_dim(private_targets, (sum_place // 2) * LANES, LANES, 0)
    line = gather_place * COLS + (sum_place % 2) * HALF
    private = lax.dynamic_slice_in_dim(rows.astype(F32).T, line, HALF, 0)
    return jnp.concatenate([shared, private], axis=0)


def own_counts(token_ids, sum_place):
    lane = lax.iota(jnp.int32, LANES)
    counts = []
    for start, lines in (
        (sum_place * LANES, COLS),
        (POOL + (sum_place // 2) * LANES, HALF),
    ):
        hits = (token_ids[:, :, None] == (start + lane)[None, None, :]).astype(F32)
        count = jnp.sum(hits, axis=1)
        counts.append(jnp.broadcast_to(count[:, None, :], (STEPS, lines, LANES)))
    return jnp.concatenate(counts, axis=1)


def on_device(
    weight,
    first_moment,
    second_moment,
    token_ids,
    shared_inputs,
    private_inputs,
    shared_targets,
    private_targets,
):
    core = lax.axis_index("core")
    z = lax.axis_index("z")
    y = lax.axis_index("y")
    sum_place = jnp.where(core == 0, z, y)
    gather_place = jnp.where(core == 0, y, z)

    slices = jnp.concatenate([shared_inputs, private_inputs[0]], axis=0).astype(F32)
    gathered = lax.all_gather(
        slices, CZY, axis=0, tiled=True, axis_index_groups=GATHER_GROUPS
    ).reshape(SIDE, TABLE, LANES)

    states = kernel_call(
        states_kernel, shaped(SIDE, 3 * COLS, LANES), weight, first_moment[0], second_moment[0]
    )
    start = exchange(states, CZY, GATHER_GROUPS)
    targets = own_targets(shared_targets, private_targets[0], sum_place, gather_place)
    counts = own_counts(token_ids[0], sum_place)

    table, parts = first_output(gathered, start)
    states = start
    for step in range(STEPS):
        parts = exchange(parts, CZY, SUM_GROUPS)
        error = kernel_call(
            functools.partial(error_kernel, step), shaped(SIDE, TILE, LANES), parts, targets, counts
        )
        error = exchange(error, CZY, SUM_GROUPS)
        last = step == STEPS - 1
        body = functools.partial(step_kernel, step == 0, last)
        if last:
            updates = kernel_call(body, shaped(SIDE, COLS, LANES), error, table, start, states)
        else:
            states, parts = kernel_call(
                body,
                [shaped(SIDE, 3 * COLS, LANES), shaped(SIDE, TILE, LANES)],
                error,
                table,
                start,
                states,
            )

    updates = exchange(updates, CZY, GATHER_GROUPS)
    turned = kernel_call(turn_kernel, shaped(REPLICAS, LANES // REPLICAS, SIDE * COLS), updates)
    updates = exchange(turned, ("x", "core"))
    gram = kernel_call(gram_kernel, shaped(REPLICAS, 1, LANES), updates)
    gram = exchange(gram, ("x", "core"))
    gram = kernel_call(gram_sum_kernel, shaped(SIDE * SIDE, 1, LANES), gram)
    gram = exchange(gram, ("z", "y"))
    return kernel_call(
        merge_kernel, shaped(LANES // REPLICAS, SIDE * COLS), gram, updates
    )


def solution(mesh):
    torus = Mesh(mesh.devices.reshape(4, 2, SIDE, SIDE), ("x", "core", "z", "y"))
    row = ("z", "y")
    rep = ("x", "core")
    placed = (
        P(row, None),
        P(rep, row, None),
        P(rep, row, None),
        P(rep, None, None),
        P(None, row),
        P(rep, None, row),
        P(),
        P(rep, None, None),
    )
    return jax.shard_map(
        on_device,
        mesh=torus,
        in_specs=placed,
        out_specs=P((*row, *rep), None),
        check_vma=False,
    )
```

```python
import functools

import jax
import jax.numpy as jnp
from jax import lax
from jax.experimental import pallas as pl
from jax.experimental.pallas import tpu as pltpu
from jax.sharding import Mesh
from jax.sharding import PartitionSpec as P

CZY = ("core", "z", "y")
F32 = jnp.float32
BF16 = jnp.bfloat16

learn_rate = 0.001
beta_one = 0.9
beta_two = 0.95
adam_eps = 1e-08
weight_decay = 0.1
norm_eps = 1e-06

SIDE = 8
LANES = 128
COLS = 48
HALF = COLS // 2
TILE = COLS + HALF
POOL = 1024
TABLE = 1536
STEPS = 4
TOKENS = 1024
REPLICAS = 8
PAIRS = [(i, j) for i in range(REPLICAS) for j in range(i, REPLICAS)]
MIB = 1024 * 1024
WIDE = 2 * LANES
OFFSETS = (0, 4, -1, 1, -2, 2, -3, 3)


def position(core, z, y):
    return (core * SIDE + z) * SIDE + y


SUM_GROUPS = [[position(0, z, y) for z in range(SIDE)] for y in range(SIDE)] + [
    [position(1, z, y) for y in range(SIDE)] for z in range(SIDE)
]
GATHER_GROUPS = [[position(0, z, y) for y in range(SIDE)] for z in range(SIDE)] + [
    [position(1, z, y) for z in range(SIDE)] for y in range(SIDE)
]


UP = [(group[i], group[(i + 1) % SIDE]) for group in GATHER_GROUPS for i in range(SIDE)]
DOWN = [(group[i], group[(i - 1) % SIDE]) for group in GATHER_GROUPS for i in range(SIDE)]


def exchange(blocks, axes, groups=None):
    return lax.all_to_all(
        blocks, axes, split_axis=0, concat_axis=0, tiled=True, axis_index_groups=groups
    )


def kernel_call(body, out_shapes, *operands, room=12):
    in_specs = [
        pl.BlockSpec(memory_space=pltpu.SMEM if operand.dtype == jnp.int32 else pltpu.VMEM)
        for operand in operands
    ]
    return pl.pallas_call(
        body,
        in_specs=in_specs,
        out_shape=out_shapes,
        compiler_params=pltpu.CompilerParams(vmem_limit_bytes=room * MIB),
    )(*operands)


def shaped(*dims, dtype=F32):
    return jax.ShapeDtypeStruct(dims, dtype)


def store_output(out_ref, output):
    for j in range(SIDE):
        out_ref[j, :COLS, :] = output[:, j * LANES : (j + 1) * LANES]
        private = POOL + (j // 2) * LANES
        line = (j % 2) * HALF
        out_ref[j, COLS:, :] = output[line : line + HALF, private : private + LANES]


def states_kernel(w_ref, m_ref, v_ref, out_ref):
    for part, ref in enumerate((w_ref, m_ref, v_ref)):
        turned = ref[...].astype(F32).T.reshape(SIDE, COLS, LANES)
        out_ref[:, part * COLS : (part + 1) * COLS, :] = turned


def widen_kernel(shared_ref, private_ref, out_ref, shared, private, arrived):
    copies = [
        pltpu.make_async_copy(shared_ref, shared, arrived.at[0]),
        pltpu.make_async_copy(private_ref, private, arrived.at[1]),
    ]
    for copy in copies:
        copy.start()
    copies[0].wait()
    out_ref[:POOL, :] = shared[...].astype(F32)
    copies[1].wait()
    out_ref[POOL:, :] = private[...].astype(F32)


def widened(shared_inputs, private_inputs):
    return pl.pallas_call(
        widen_kernel,
        in_specs=[pl.BlockSpec(memory_space=pltpu.HBM)] * 2,
        out_shape=shaped(TABLE, LANES),
        scratch_shapes=[
            pltpu.VMEM((POOL, LANES), BF16),
            pltpu.VMEM((TABLE - POOL, LANES), BF16),
            pltpu.SemaphoreType.DMA((2,)),
        ],
        compiler_params=pltpu.CompilerParams(vmem_limit_bytes=4 * MIB),
    )(shared_inputs, private_inputs)


def narrow_kernel(*refs):
    *blocks, out_ref = refs
    for k, block in enumerate(blocks):
        out_ref[:, k * LANES : (k + 1) * LANES] = block[...].astype(BF16)


def narrowed(*blocks):
    return kernel_call(narrow_kernel, shaped(TABLE, len(blocks) * LANES, dtype=BF16), *blocks)


def turned_product(weights, table_rows):
    return lax.dot_general(
        weights, table_rows, (((1,), (1,)), ((), ())), preferred_element_type=F32
    )


def early_kernel(
    place_ref, start_ref, target_ref, count_ref, own_ref, *refs
):
    pairs, (states_ref, constant_ref, part_ref) = refs[:3], refs[3:]
    place = place_ref[0]
    for k, offset in enumerate(OFFSETS):
        states_ref[k] = start_ref[lax.rem(place + (offset + SIDE), SIDE)]
    constant_ref[:STEPS] = count_ref[...]
    constant_ref[STEPS] = target_ref[...]
    weights = [states_ref[k, :COLS, :].astype(BF16) for k in range(SIDE)]
    for row in range(0, TABLE, WIDE):
        rows = slice(row, row + WIDE)
        part = turned_product(weights[0], own_ref[rows, :])
        for k, pair in enumerate(pairs):
            both = jnp.concatenate(weights[2 * k + 2 : 2 * k + 4], axis=1)
            part = part + turned_product(both, pair[rows, :])
        part_ref[:, rows] = part


def late_kernel(states_ref, own_ref, opposite_ref, part_ref, table_ref, out_ref):
    table_ref[:, :LANES] = own_ref[...]
    table_ref[:, LANES:] = opposite_ref[...].astype(BF16)
    weights = states_ref[1, :COLS, :].astype(BF16)
    output = jnp.concatenate(
        [
            part_ref[:, row : row + WIDE]
            + turned_product(weights, table_ref[row : row + WIDE, LANES:])
            for row in range(0, TABLE, WIDE)
        ],
        axis=1,
    )
    store_output(out_ref, output)


def error_kernel(step, parts_ref, constant_ref, out_ref):
    output = parts_ref[0]
    for j in range(1, SIDE):
        output = output + parts_ref[j]
    error = (output - constant_ref[STEPS]).astype(BF16).astype(F32)
    weighted = error * constant_ref[step]
    for j in range(SIDE):
        out_ref[j] = weighted


def step_kernel(first, last, place_ref, error_ref, *refs):
    tables, (w_ref, states_ref, *rest) = refs[: SIDE // 2], refs[SIDE // 2 :]
    if last:
        (total_out,) = rest
        place = place_ref[0]
    else:
        new_states, output_ref = rest
    error = jnp.concatenate(
        [error_ref[j, :COLS, :] for j in range(SIDE)]
        + [
            jnp.concatenate([error_ref[2 * k, COLS:, :], error_ref[2 * k + 1, COLS:, :]], axis=0)
            for k in range(SIDE // 2)
        ],
        axis=1,
    )
    high = error.astype(BF16)
    low = (error - high.astype(F32)).astype(BF16)
    both = jnp.concatenate([high, low], axis=0)
    updated = []
    for k in range(SIDE // 2):
        product = jnp.dot(both, tables[k][...], preferred_element_type=F32)
        gradients = (product[:COLS] + product[COLS:]) * (1.0 / TOKENS)
        for half in range(2):
            j = 2 * k + half
            gradient = gradients[:, half * LANES : (half + 1) * LANES]
            weight_start = w_ref[j, :COLS, :]
            if first:
                weight_now = weight_start
            else:
                update_sum = states_ref[j, 2 * COLS :, :]
                weight_now = weight_start - learn_rate * update_sum
            base = COLS if first else 0
            moment_one = states_ref[j, base : base + COLS, :]
            moment_two = states_ref[j, base + COLS : base + 2 * COLS, :]
            moment_one = beta_one * moment_one + (1.0 - beta_one) * gradient
            moment_two = beta_two * moment_two + (1.0 - beta_two) * gradient * gradient
            direction = (
                moment_one / (jnp.sqrt(moment_two) + adam_eps) + weight_decay * weight_now
            )
            update_sum = direction if first else update_sum + direction
            if last:
                total_out[lax.rem(place + (OFFSETS[j] + SIDE), SIDE)] = update_sum
            else:
                new_states[j, :COLS, :] = moment_one
                new_states[j, COLS : 2 * COLS, :] = moment_two
                new_states[j, 2 * COLS :, :] = update_sum
                updated.append((weight_start - learn_rate * update_sum).astype(BF16))
    if last:
        return
    weights = jnp.concatenate(updated, axis=1)
    output = []
    for row in range(0, TABLE, WIDE):
        rows = slice(row, row + WIDE)
        table_rows = jnp.concatenate([table[rows, :] for table in tables], axis=1)
        output.append(turned_product(weights, table_rows))
    store_output(output_ref, jnp.concatenate(output, axis=1))


def turn_kernel(parts_ref, out_ref):
    turned = parts_ref[...].reshape(SIDE * COLS, LANES).T
    out_ref[...] = turned.reshape(REPLICAS, LANES // REPLICAS, SIDE * COLS)


def gram_kernel(updates_ref, out_ref):
    updates = [updates_ref[r] for r in range(REPLICAS)]
    lines = []
    for i, j in PAIRS:
        product = updates[i] * updates[j]
        lines.append(jnp.sum(product, axis=0, keepdims=True))
    while len(lines) % 8:
        lines.append(jnp.zeros_like(lines[0]))
    sums = jnp.sum(jnp.concatenate(lines, axis=0), axis=1, keepdims=True)
    spread = jnp.broadcast_to(sums, (len(lines), LANES))
    line = lax.broadcasted_iota(jnp.int32, spread.shape, 0)
    lane = lax.broadcasted_iota(jnp.int32, spread.shape, 1)
    packed = jnp.sum(jnp.where(line == lane, spread, 0.0), axis=0, keepdims=True)
    for j in range(REPLICAS):
        out_ref[j] = packed


def gram_sum_kernel(parts_ref, out_ref):
    packed = jnp.sum(parts_ref[...], axis=0)
    for j in range(SIDE * SIDE):
        out_ref[j] = packed


def merge_kernel(parts_ref, updates_ref, out_ref):
    packed = jnp.sum(parts_ref[...], axis=0)
    lane = lax.broadcasted_iota(jnp.int32, packed.shape, 1)
    gram = {}
    for place, (i, j) in enumerate(PAIRS):
        value = jnp.sum(jnp.where(lane == place, packed, 0.0), axis=1, keepdims=True)
        gram[i, j] = value
        gram[j, i] = value
    members = [[r] for r in range(REPLICAS)]
    while len(members) > 1:
        merged = []
        for lower, upper in zip(members[0::2], members[1::2]):
            cross_dot = sum(gram[i, j] for i in lower for j in upper)
            lower_norm = sum(gram[i, j] for i in lower for j in lower)
            upper_norm = sum(gram[i, j] for i in upper for j in upper)
            lower_coef = 1.0 - cross_dot / (2.0 * (lower_norm + norm_eps))
            upper_coef = 1.0 - cross_dot / (2.0 * (upper_norm + norm_eps))
            scale = {**{i: lower_coef for i in lower}, **{i: upper_coef for i in upper}}
            merged.append((lower + upper, scale))
        factor = {i: scale[i] for _, scale in merged for i in scale}
        gram = {(i, j): factor[i] * factor[j] * value for (i, j), value in gram.items()}
        total = factor if len(merged) * 2 == REPLICAS else {i: total[i] * factor[i] for i in total}
        members = [group for group, _ in merged]
    result = total[0] * updates_ref[0]
    for r in range(1, REPLICAS):
        result = result + total[r] * updates_ref[r]
    out_ref[...] = result


def own_targets(shared_targets, private_targets, sum_place, gather_place):
    rows = lax.dynamic_slice_in_dim(shared_targets, sum_place * LANES, LANES, 0)
    shared = lax.dynamic_slice_in_dim(rows.astype(F32).T, gather_place * COLS, COLS, 0)
    rows = lax.dynamic_slice_in_dim(private_targets, (sum_place // 2) * LANES, LANES, 0)
    line = gather_place * COLS + (sum_place % 2) * HALF
    private = lax.dynamic_slice_in_dim(rows.astype(F32).T, line, HALF, 0)
    return jnp.concatenate([shared, private], axis=0)


def own_counts(token_ids, sum_place):
    lane = lax.iota(jnp.int32, LANES)
    counts = []
    for start, lines in (
        (sum_place * LANES, COLS),
        (POOL + (sum_place // 2) * LANES, HALF),
    ):
        hits = (token_ids[:, :, None] == (start + lane)[None, None, :]).astype(F32)
        count = jnp.sum(hits, axis=1)
        counts.append(jnp.broadcast_to(count[:, None, :], (STEPS, lines, LANES)))
    return jnp.concatenate(counts, axis=1)


def on_device(
    weight,
    first_moment,
    second_moment,
    token_ids,
    shared_inputs,
    private_inputs,
    shared_targets,
    private_targets,
):
    core = lax.axis_index("core")
    z = lax.axis_index("z")
    y = lax.axis_index("y")
    sum_place = jnp.where(core == 0, z, y)
    gather_place = jnp.where(core == 0, y, z)

    own = widened(shared_inputs, private_inputs[0])
    tables = [narrowed(own)]
    upward = downward = own
    for hop in range(3):
        if hop >= 1:
            upward, tables[hop - 1] = lax.optimization_barrier((upward, tables[hop - 1]))
        upward = lax.ppermute(upward, CZY, UP)
        downward = lax.ppermute(downward, CZY, DOWN)
        tables.append(narrowed(upward, downward))
    opposite, tables[2] = lax.optimization_barrier((upward, tables[2]))
    opposite = lax.ppermute(opposite, CZY, UP)

    start = kernel_call(
        states_kernel, shaped(SIDE, 3 * COLS, LANES), weight, first_moment[0], second_moment[0]
    )
    start = exchange(start, CZY, GATHER_GROUPS)
    targets = own_targets(shared_targets, private_targets[0], sum_place, gather_place)
    counts = own_counts(token_ids[0], sum_place)
    place = gather_place.astype(jnp.int32).reshape(1)

    start, constants, part = kernel_call(
        early_kernel,
        [
            shaped(SIDE, 3 * COLS, LANES),
            shaped(STEPS + 1, TILE, LANES),
            shaped(COLS, TABLE),
        ],
        place,
        start,
        targets,
        counts,
        *tables,
    )
    tables[0], parts = kernel_call(
        late_kernel,
        [shaped(TABLE, WIDE, dtype=BF16), shaped(SIDE, TILE, LANES)],
        start,
        tables[0],
        opposite,
        part,
    )
    states = start
    for step in range(STEPS):
        parts = exchange(parts, CZY, SUM_GROUPS)
        error = kernel_call(
            functools.partial(error_kernel, step), shaped(SIDE, TILE, LANES), parts, constants
        )
        error = exchange(error, CZY, SUM_GROUPS)
        last = step == STEPS - 1
        body = functools.partial(step_kernel, step == 0, last)
        operands = (place, error, *tables, start, states)
        if last:
            updates = kernel_call(body, shaped(SIDE, COLS, LANES), *operands)
        else:
            states, parts = kernel_call(
                body, [shaped(SIDE, 3 * COLS, LANES), shaped(SIDE, TILE, LANES)], *operands
            )

    updates = exchange(updates, CZY, GATHER_GROUPS)
    turned = kernel_call(turn_kernel, shaped(REPLICAS, LANES // REPLICAS, SIDE * COLS), updates)
    updates = exchange(turned, ("x", "core"))
    gram = kernel_call(gram_kernel, shaped(REPLICAS, 1, LANES), updates)
    gram = exchange(gram, ("x", "core"))
    gram = kernel_call(gram_sum_kernel, shaped(SIDE * SIDE, 1, LANES), gram)
    gram = exchange(gram, ("z", "y"))
    return kernel_call(
        merge_kernel, shaped(LANES // REPLICAS, SIDE * COLS), gram, updates
    )


def solution(mesh):
    torus = Mesh(mesh.devices.reshape(4, 2, SIDE, SIDE), ("x", "core", "z", "y"))
    row = ("z", "y")
    rep = ("x", "core")
    placed = (
        P(row, None),
        P(rep, row, None),
        P(rep, row, None),
        P(rep, None, None),
        P(None, row),
        P(rep, None, row),
        P(),
        P(rep, None, None),
    )
    return jax.shard_map(
        on_device,
        mesh=torus,
        in_specs=placed,
        out_specs=P((*row, *rep), None),
        check_vma=False,
    )
```

```python
import functools

import jax
import jax.numpy as jnp
from jax import lax
from jax.experimental import pallas as pl
from jax.experimental.pallas import tpu as pltpu
from jax.sharding import Mesh
from jax.sharding import PartitionSpec as P

CZY = ("core", "z", "y")
F32 = jnp.float32
BF16 = jnp.bfloat16

learn_rate = 0.001
beta_one = 0.9
beta_two = 0.95
adam_eps = 1e-08
weight_decay = 0.1
norm_eps = 1e-06

SIDE = 8
LANES = 128
COLS = 48
HALF = COLS // 2
TILE = COLS + HALF
POOL = 1024
TABLE = 1536
STEPS = 4
TOKENS = 1024
REPLICAS = 8
PAIRS = [(i, j) for i in range(REPLICAS) for j in range(i, REPLICAS)]
MIB = 1024 * 1024
WIDE = 2 * LANES
OFFSETS = (0, 4, -1, 1, -2, 2, -3, 3)


def position(core, z, y):
    return (core * SIDE + z) * SIDE + y


SUM_GROUPS = [[position(0, z, y) for z in range(SIDE)] for y in range(SIDE)] + [
    [position(1, z, y) for y in range(SIDE)] for z in range(SIDE)
]
GATHER_GROUPS = [[position(0, z, y) for y in range(SIDE)] for z in range(SIDE)] + [
    [position(1, z, y) for z in range(SIDE)] for y in range(SIDE)
]


UP = [(group[i], group[(i + 1) % SIDE]) for group in GATHER_GROUPS for i in range(SIDE)]
DOWN = [(group[i], group[(i - 1) % SIDE]) for group in GATHER_GROUPS for i in range(SIDE)]
ACROSS = [(group[i], group[(i + 4) % SIDE]) for group in GATHER_GROUPS for i in range(SIDE)]


def exchange(blocks, axes, groups=None):
    return lax.all_to_all(
        blocks, axes, split_axis=0, concat_axis=0, tiled=True, axis_index_groups=groups
    )


def kernel_call(body, out_shapes, *operands, room=12):
    in_specs = [
        pl.BlockSpec(memory_space=pltpu.SMEM if operand.dtype == jnp.int32 else pltpu.VMEM)
        for operand in operands
    ]
    return pl.pallas_call(
        body,
        in_specs=in_specs,
        out_shape=out_shapes,
        compiler_params=pltpu.CompilerParams(vmem_limit_bytes=room * MIB),
    )(*operands)


def shaped(*dims, dtype=F32):
    return jax.ShapeDtypeStruct(dims, dtype)


def store_output(out_ref, output):
    for j in range(SIDE):
        out_ref[j, :COLS, :] = output[:, j * LANES : (j + 1) * LANES]
        private = POOL + (j // 2) * LANES
        line = (j % 2) * HALF
        out_ref[j, COLS:, :] = output[line : line + HALF, private : private + LANES]


def states_kernel(w_ref, m_ref, v_ref, out_ref):
    for part, ref in enumerate((w_ref, m_ref, v_ref)):
        turned = ref[...].astype(F32).T.reshape(SIDE, COLS, LANES)
        out_ref[:, part * COLS : (part + 1) * COLS, :] = turned


def widen_kernel(shared_ref, private_ref, out_ref, shared, private, arrived):
    copies = [
        pltpu.make_async_copy(shared_ref, shared, arrived.at[0]),
        pltpu.make_async_copy(private_ref, private, arrived.at[1]),
    ]
    for copy in copies:
        copy.start()
    copies[0].wait()
    out_ref[:POOL, :] = shared[...].astype(F32)
    copies[1].wait()
    out_ref[POOL:, :] = private[...].astype(F32)


def widened(shared_inputs, private_inputs):
    return pl.pallas_call(
        widen_kernel,
        in_specs=[pl.BlockSpec(memory_space=pltpu.HBM)] * 2,
        out_shape=shaped(TABLE, LANES),
        scratch_shapes=[
            pltpu.VMEM((POOL, LANES), BF16),
            pltpu.VMEM((TABLE - POOL, LANES), BF16),
            pltpu.SemaphoreType.DMA((2,)),
        ],
        compiler_params=pltpu.CompilerParams(vmem_limit_bytes=4 * MIB),
    )(shared_inputs, private_inputs)


def narrow_kernel(*refs):
    *blocks, out_ref = refs
    for k, block in enumerate(blocks):
        out_ref[:, k * LANES : (k + 1) * LANES] = block[...].astype(BF16)


def narrowed(*blocks):
    return kernel_call(narrow_kernel, shaped(TABLE, len(blocks) * LANES, dtype=BF16), *blocks)


def turned_product(weights, table_rows):
    return lax.dot_general(
        weights, table_rows, (((1,), (1,)), ((), ())), preferred_element_type=F32
    )


def early_kernel(
    place_ref, start_ref, target_ref, count_ref, own_ref, *refs
):
    pairs, (states_ref, constant_ref, part_ref) = refs[:2], refs[2:]
    place = place_ref[0]
    for k, offset in enumerate(OFFSETS):
        states_ref[k] = start_ref[lax.rem(place + (offset + SIDE), SIDE)]
    constant_ref[:STEPS] = count_ref[...]
    constant_ref[STEPS] = target_ref[...]
    weights = [states_ref[k, :COLS, :].astype(BF16) for k in range(SIDE)]
    for row in range(0, TABLE, WIDE):
        rows = slice(row, row + WIDE)
        part = turned_product(weights[0], own_ref[rows, :])
        for k, pair in enumerate(pairs):
            both = jnp.concatenate(weights[2 * k + 2 : 2 * k + 4], axis=1)
            part = part + turned_product(both, pair[rows, :])
        part_ref[:, rows] = part


def late_kernel(
    states_ref, upward_ref, downward_ref, opposite_ref, part_ref, pair_ref, single_ref, out_ref
):
    pair_ref[:, :LANES] = upward_ref[...].astype(BF16)
    pair_ref[:, LANES:] = downward_ref[...].astype(BF16)
    single_ref[...] = opposite_ref[...].astype(BF16)
    weights = jnp.concatenate([states_ref[k, :COLS, :] for k in (6, 7)], axis=1).astype(BF16)
    single = states_ref[1, :COLS, :].astype(BF16)
    output = []
    for row in range(0, TABLE, WIDE):
        rows = slice(row, row + WIDE)
        part = part_ref[:, rows] + turned_product(weights, pair_ref[rows, :])
        output.append(part + turned_product(single, single_ref[rows, :]))
    store_output(out_ref, jnp.concatenate(output, axis=1))


def error_kernel(step, parts_ref, constant_ref, out_ref):
    output = parts_ref[0]
    for j in range(1, SIDE):
        output = output + parts_ref[j]
    error = (output - constant_ref[STEPS]).astype(BF16).astype(F32)
    weighted = error * constant_ref[step]
    for j in range(SIDE):
        out_ref[j] = weighted


def step_kernel(first, last, place_ref, error_ref, *refs):
    own, opposite, *pairs = refs[:5]
    w_ref, states_ref, *rest = refs[5:]
    if last:
        (total_out,) = rest
        place = place_ref[0]
    else:
        new_states, output_ref = rest
    error = jnp.concatenate(
        [error_ref[j, :COLS, :] for j in range(SIDE)]
        + [
            jnp.concatenate([error_ref[2 * k, COLS:, :], error_ref[2 * k + 1, COLS:, :]], axis=0)
            for k in range(SIDE // 2)
        ],
        axis=1,
    )
    high = error.astype(BF16)
    low = (error - high.astype(F32)).astype(BF16)
    both = jnp.concatenate([high, low], axis=0)
    updated = []
    for k in range(SIDE // 2):
        if k == 0:
            columns = jnp.concatenate([own[...], opposite[...]], axis=1)
        else:
            columns = pairs[k - 1][...]
        product = jnp.dot(both, columns, preferred_element_type=F32)
        gradients = (product[:COLS] + product[COLS:]) * (1.0 / TOKENS)
        for half in range(2):
            j = 2 * k + half
            gradient = gradients[:, half * LANES : (half + 1) * LANES]
            weight_start = w_ref[j, :COLS, :]
            if first:
                weight_now = weight_start
            else:
                update_sum = states_ref[j, 2 * COLS :, :]
                weight_now = weight_start - learn_rate * update_sum
            base = COLS if first else 0
            moment_one = states_ref[j, base : base + COLS, :]
            moment_two = states_ref[j, base + COLS : base + 2 * COLS, :]
            moment_one = beta_one * moment_one + (1.0 - beta_one) * gradient
            moment_two = beta_two * moment_two + (1.0 - beta_two) * gradient * gradient
            direction = (
                moment_one / (jnp.sqrt(moment_two) + adam_eps) + weight_decay * weight_now
            )
            update_sum = direction if first else update_sum + direction
            if last:
                total_out[lax.rem(place + (OFFSETS[j] + SIDE), SIDE)] = update_sum
            else:
                new_states[j, :COLS, :] = moment_one
                new_states[j, COLS : 2 * COLS, :] = moment_two
                new_states[j, 2 * COLS :, :] = update_sum
                updated.append((weight_start - learn_rate * update_sum).astype(BF16))
    if last:
        return
    weights = jnp.concatenate(updated, axis=1)
    output = []
    for row in range(0, TABLE, WIDE):
        rows = slice(row, row + WIDE)
        table_rows = jnp.concatenate([table[rows, :] for table in refs[:5]], axis=1)
        output.append(turned_product(weights, table_rows))
    store_output(output_ref, jnp.concatenate(output, axis=1))


def turn_kernel(parts_ref, out_ref):
    turned = parts_ref[...].reshape(SIDE * COLS, LANES).T
    out_ref[...] = turned.reshape(REPLICAS, LANES // REPLICAS, SIDE * COLS)


def gram_kernel(updates_ref, out_ref):
    updates = [updates_ref[r] for r in range(REPLICAS)]
    lines = []
    for i, j in PAIRS:
        product = updates[i] * updates[j]
        lines.append(jnp.sum(product, axis=0, keepdims=True))
    while len(lines) % 8:
        lines.append(jnp.zeros_like(lines[0]))
    sums = jnp.sum(jnp.concatenate(lines, axis=0), axis=1, keepdims=True)
    spread = jnp.broadcast_to(sums, (len(lines), LANES))
    line = lax.broadcasted_iota(jnp.int32, spread.shape, 0)
    lane = lax.broadcasted_iota(jnp.int32, spread.shape, 1)
    packed = jnp.sum(jnp.where(line == lane, spread, 0.0), axis=0, keepdims=True)
    for j in range(REPLICAS):
        out_ref[j] = packed


def gram_sum_kernel(parts_ref, out_ref):
    packed = jnp.sum(parts_ref[...], axis=0)
    for j in range(SIDE * SIDE):
        out_ref[j] = packed


def merge_kernel(parts_ref, updates_ref, out_ref):
    packed = jnp.sum(parts_ref[...], axis=0)
    lane = lax.broadcasted_iota(jnp.int32, packed.shape, 1)
    gram = {}
    for place, (i, j) in enumerate(PAIRS):
        value = jnp.sum(jnp.where(lane == place, packed, 0.0), axis=1, keepdims=True)
        gram[i, j] = value
        gram[j, i] = value
    members = [[r] for r in range(REPLICAS)]
    while len(members) > 1:
        merged = []
        for lower, upper in zip(members[0::2], members[1::2]):
            cross_dot = sum(gram[i, j] for i in lower for j in upper)
            lower_norm = sum(gram[i, j] for i in lower for j in lower)
            upper_norm = sum(gram[i, j] for i in upper for j in upper)
            lower_coef = 1.0 - cross_dot / (2.0 * (lower_norm + norm_eps))
            upper_coef = 1.0 - cross_dot / (2.0 * (upper_norm + norm_eps))
            scale = {**{i: lower_coef for i in lower}, **{i: upper_coef for i in upper}}
            merged.append((lower + upper, scale))
        factor = {i: scale[i] for _, scale in merged for i in scale}
        gram = {(i, j): factor[i] * factor[j] * value for (i, j), value in gram.items()}
        total = factor if len(merged) * 2 == REPLICAS else {i: total[i] * factor[i] for i in total}
        members = [group for group, _ in merged]
    result = total[0] * updates_ref[0]
    for r in range(1, REPLICAS):
        result = result + total[r] * updates_ref[r]
    out_ref[...] = result


def own_targets(shared_targets, private_targets, sum_place, gather_place):
    rows = lax.dynamic_slice_in_dim(shared_targets, sum_place * LANES, LANES, 0)
    shared = lax.dynamic_slice_in_dim(rows.astype(F32).T, gather_place * COLS, COLS, 0)
    rows = lax.dynamic_slice_in_dim(private_targets, (sum_place // 2) * LANES, LANES, 0)
    line = gather_place * COLS + (sum_place % 2) * HALF
    private = lax.dynamic_slice_in_dim(rows.astype(F32).T, line, HALF, 0)
    return jnp.concatenate([shared, private], axis=0)


def own_counts(token_ids, sum_place):
    lane = lax.iota(jnp.int32, LANES)
    counts = []
    for start, lines in (
        (sum_place * LANES, COLS),
        (POOL + (sum_place // 2) * LANES, HALF),
    ):
        hits = (token_ids[:, :, None] == (start + lane)[None, None, :]).astype(F32)
        count = jnp.sum(hits, axis=1)
        counts.append(jnp.broadcast_to(count[:, None, :], (STEPS, lines, LANES)))
    return jnp.concatenate(counts, axis=1)


def on_device(
    weight,
    first_moment,
    second_moment,
    token_ids,
    shared_inputs,
    private_inputs,
    shared_targets,
    private_targets,
):
    core = lax.axis_index("core")
    z = lax.axis_index("z")
    y = lax.axis_index("y")
    sum_place = jnp.where(core == 0, z, y)
    gather_place = jnp.where(core == 0, y, z)

    own = widened(shared_inputs, private_inputs[0])
    own_table = narrowed(own)
    tables = []
    upward = downward = own
    for hop in range(3):
        if hop >= 2:
            upward, tables[hop - 2] = lax.optimization_barrier((upward, tables[hop - 2]))
        upward = lax.ppermute(upward, CZY, UP)
        downward = lax.ppermute(downward, CZY, DOWN)
        if hop == 0:
            opposite = lax.ppermute(own, CZY, ACROSS)
        tables.append(narrowed(upward, downward) if hop < 2 else None)

    start = kernel_call(
        states_kernel, shaped(SIDE, 3 * COLS, LANES), weight, first_moment[0], second_moment[0]
    )
    start = exchange(start, CZY, GATHER_GROUPS)
    targets = own_targets(shared_targets, private_targets[0], sum_place, gather_place)
    counts = own_counts(token_ids[0], sum_place)
    place = gather_place.astype(jnp.int32).reshape(1)

    start, constants, part = kernel_call(
        early_kernel,
        [
            shaped(SIDE, 3 * COLS, LANES),
            shaped(STEPS + 1, TILE, LANES),
            shaped(COLS, TABLE),
        ],
        place,
        start,
        targets,
        counts,
        own_table,
        *tables[:2],
    )
    tables[2], opposite, parts = kernel_call(
        late_kernel,
        [
            shaped(TABLE, WIDE, dtype=BF16),
            shaped(TABLE, LANES, dtype=BF16),
            shaped(SIDE, TILE, LANES),
        ],
        start,
        upward,
        downward,
        opposite,
        part,
    )
    states = start
    for step in range(STEPS):
        parts = exchange(parts, CZY, SUM_GROUPS)
        error = kernel_call(
            functools.partial(error_kernel, step), shaped(SIDE, TILE, LANES), parts, constants
        )
        error = exchange(error, CZY, SUM_GROUPS)
        last = step == STEPS - 1
        body = functools.partial(step_kernel, step == 0, last)
        operands = (place, error, own_table, opposite, *tables, start, states)
        if last:
            updates = kernel_call(body, shaped(SIDE, COLS, LANES), *operands)
        else:
            states, parts = kernel_call(
                body, [shaped(SIDE, 3 * COLS, LANES), shaped(SIDE, TILE, LANES)], *operands
            )

    updates = exchange(updates, CZY, GATHER_GROUPS)
    turned = kernel_call(turn_kernel, shaped(REPLICAS, LANES // REPLICAS, SIDE * COLS), updates)
    updates = exchange(turned, ("x", "core"))
    gram = kernel_call(gram_kernel, shaped(REPLICAS, 1, LANES), updates)
    gram = exchange(gram, ("x", "core"))
    gram = kernel_call(gram_sum_kernel, shaped(SIDE * SIDE, 1, LANES), gram)
    gram = exchange(gram, ("z", "y"))
    return kernel_call(
        merge_kernel, shaped(LANES // REPLICAS, SIDE * COLS), gram, updates
    )


def solution(mesh):
    torus = Mesh(mesh.devices.reshape(4, 2, SIDE, SIDE), ("x", "core", "z", "y"))
    row = ("z", "y")
    rep = ("x", "core")
    placed = (
        P(row, None),
        P(rep, row, None),
        P(rep, row, None),
        P(rep, None, None),
        P(None, row),
        P(rep, None, row),
        P(),
        P(rep, None, None),
    )
    return jax.shard_map(
        on_device,
        mesh=torus,
        in_specs=placed,
        out_specs=P((*row, *rep), None),
        check_vma=False,
    )
```

```python
import functools

import jax
import jax.numpy as jnp
from jax import lax
from jax.experimental import pallas as pl
from jax.experimental.pallas import tpu as pltpu
from jax.sharding import Mesh
from jax.sharding import PartitionSpec as P

CZY = ("core", "z", "y")
F32 = jnp.float32
BF16 = jnp.bfloat16

learn_rate = 0.001
beta_one = 0.9
beta_two = 0.95
adam_eps = 1e-08
weight_decay = 0.1
norm_eps = 1e-06

SIDE = 8
LANES = 128
COLS = 48
HALF = COLS // 2
STATE = 3 * COLS
TILE = COLS + HALF
POOL = 1024
TABLE = 1536
STEPS = 4
TOKENS = 1024
REPLICAS = 8
PAIRS = [(i, j) for i in range(REPLICAS) for j in range(i, REPLICAS)]
MIB = 1024 * 1024
WIDE = 2 * LANES


def position(core, z, y):
    return (core * SIDE + z) * SIDE + y


SUM_GROUPS = [[position(0, z, y) for z in range(SIDE)] for y in range(SIDE)] + [
    [position(1, z, y) for y in range(SIDE)] for z in range(SIDE)
]
GATHER_GROUPS = [[position(0, z, y) for y in range(SIDE)] for z in range(SIDE)] + [
    [position(1, z, y) for z in range(SIDE)] for y in range(SIDE)
]


def exchange(blocks, axes, groups=None):
    return lax.all_to_all(
        blocks, axes, split_axis=0, concat_axis=0, tiled=True, axis_index_groups=groups
    )


def kernel_call(body, out_shapes, *operands, room=12):
    in_specs = [
        pl.BlockSpec(memory_space=pltpu.SMEM if operand.dtype == jnp.int32 else pltpu.VMEM)
        for operand in operands
    ]
    return pl.pallas_call(
        body,
        in_specs=in_specs,
        out_shape=out_shapes,
        compiler_params=pltpu.CompilerParams(vmem_limit_bytes=room * MIB),
    )(*operands)


def shaped(*dims, dtype=F32):
    return jax.ShapeDtypeStruct(dims, dtype)


def store_output(out_ref, output):
    for j in range(SIDE):
        out_ref[j, :COLS, :] = output[:, j * LANES : (j + 1) * LANES]
        private = POOL + (j // 2) * LANES
        line = (j % 2) * HALF
        out_ref[j, COLS:, :] = output[line : line + HALF, private : private + LANES]


def turned_product(left, right):
    return lax.dot_general(left, right, (((1,), (1,)), ((), ())), preferred_element_type=F32)


def whole_error(error_ref):
    error = jnp.concatenate(
        [error_ref[j, :COLS, :] for j in range(SIDE)]
        + [
            jnp.concatenate([error_ref[2 * k, COLS:, :], error_ref[2 * k + 1, COLS:, :]], axis=0)
            for k in range(SIDE // 2)
        ],
        axis=1,
    )
    high = error.astype(BF16)
    low = (error - high.astype(F32)).astype(BF16)
    return jnp.concatenate([high, low], axis=0)


def stepped(gradient, weight_start, moment_one, moment_two, update_sum):
    if update_sum is None:
        weight_now = weight_start
    else:
        weight_now = weight_start - learn_rate * update_sum
    moment_one = beta_one * moment_one + (1.0 - beta_one) * gradient
    moment_two = beta_two * moment_two + (1.0 - beta_two) * gradient * gradient
    direction = moment_one / (jnp.sqrt(moment_two) + adam_eps) + weight_decay * weight_now
    update_sum = direction if update_sum is None else update_sum + direction
    return moment_one, moment_two, update_sum


def widen_kernel(shared_ref, private_ref, out_ref):
    out_ref[:POOL, :] = shared_ref[...].astype(F32)
    out_ref[POOL:, :] = private_ref[...].astype(F32)


def own_kernel(slice_ref, weight_ref, out_ref):
    weights = weight_ref[...].astype(F32).T.astype(BF16)
    own = slice_ref[...].astype(BF16)
    for i in range(SIDE):
        shared = turned_product(weights, own[i * LANES : (i + 1) * LANES, :])
        for j in range(SIDE):
            out_ref[i, j * TILE : j * TILE + COLS, :] = shared[j * COLS : (j + 1) * COLS, :]
    for k in range(SIDE // 2):
        row = POOL + k * LANES
        private = turned_product(weights, own[row : row + LANES, :])
        for j in range(SIDE):
            for half in range(2):
                line = j * COLS + half * HALF
                place = j * TILE + COLS
                out_ref[2 * k + half, place : place + HALF, :] = private[line : line + HALF, :]


def constant_kernel(place_ref, ids_ref, shared_ref, private_ref, out_ref, rows, turned, arrived):
    i, j = place_ref[0], place_ref[1]
    shared_rows = pl.ds(pl.multiple_of(i * LANES, LANES), LANES)
    private_rows = pl.ds(pl.multiple_of(lax.div(i, 2) * LANES, LANES), LANES)
    copies = [
        pltpu.make_async_copy(shared_ref.at[shared_rows], rows.at[0], arrived.at[0]),
        pltpu.make_async_copy(private_ref.at[private_rows], rows.at[1], arrived.at[1]),
    ]
    for copy in copies:
        copy.start()
    row = lax.broadcasted_iota(jnp.int32, (LANES, TOKENS), 0)
    ones = jnp.ones((16, TOKENS), BF16)
    for start, lines in (
        (i * LANES, slice(0, COLS)),
        (POOL + lax.div(i, 2) * LANES, slice(COLS, TILE)),
    ):
        for step in range(STEPS):
            hits = jnp.where(ids_ref[step : step + 1, :] == row + start, 1.0, 0.0).astype(BF16)
            count = turned_product(ones, hits)[:1]
            out_ref[step, lines, :] = jnp.broadcast_to(count, (lines.stop - lines.start, LANES))
    for copy in copies:
        copy.wait()
    turned[...] = rows[0].astype(F32).T
    columns = pl.ds(pl.multiple_of(j * COLS, 8), COLS)
    out_ref[STEPS, :COLS, :] = turned[columns, :]
    turned[...] = rows[1].astype(F32).T
    columns = pl.ds(pl.multiple_of(j * COLS + lax.rem(i, 2) * HALF, 8), HALF)
    out_ref[STEPS, COLS:, :] = turned[columns, :]


def own_constants(places, ids, shared_targets, private_targets):
    return pl.pallas_call(
        constant_kernel,
        in_specs=[
            pl.BlockSpec(memory_space=pltpu.SMEM),
            pl.BlockSpec(memory_space=pltpu.VMEM),
            pl.BlockSpec(memory_space=pl.ANY),
            pl.BlockSpec(memory_space=pl.ANY),
        ],
        out_shape=shaped(STEPS + 1, TILE, LANES),
        scratch_shapes=[
            pltpu.VMEM((2, LANES, SIDE * COLS), BF16),
            pltpu.VMEM((SIDE * COLS, LANES), F32),
            pltpu.SemaphoreType.DMA((2,)),
        ],
        compiler_params=pltpu.CompilerParams(vmem_limit_bytes=8 * MIB),
    )(places, ids, shared_targets, private_targets)


def between_kernel(parts_ref, w_ref, m_ref, v_ref, out_ref):
    for part, ref in enumerate((w_ref, m_ref, v_ref)):
        turned = ref[...].astype(F32).T.reshape(SIDE, COLS, LANES)
        out_ref[:, part * COLS : (part + 1) * COLS, :] = turned
    for j in range(SIDE):
        lines = slice(j * TILE, (j + 1) * TILE)
        output = parts_ref[0, lines, :]
        for source in range(1, SIDE):
            output = output + parts_ref[source, lines, :]
        out_ref[j, STATE:, :] = output


def first_kernel(
    gathered_ref, error_ref, start_ref, table_ref, states_ref, output_ref, slices, arrived
):
    copies = [
        pltpu.make_async_copy(gathered_ref.at[j], slices.at[j], arrived.at[j]) for j in range(SIDE)
    ]
    for copy in copies:
        copy.start()
    both = whole_error(error_ref)
    total = None
    for k in range(SIDE // 2):
        copies[2 * k].wait()
        copies[2 * k + 1].wait()
        pair = jnp.concatenate([slices[2 * k], slices[2 * k + 1]], axis=1).astype(BF16)
        columns = slice(k * WIDE, (k + 1) * WIDE)
        table_ref[:, columns] = pair
        product = jnp.dot(both, table_ref[:, columns], preferred_element_type=F32)
        gradients = (product[:COLS] + product[COLS:]) * (1.0 / TOKENS)
        weights = []
        for half in range(2):
            j = 2 * k + half
            weight_start = start_ref[j, :COLS, :]
            moment_one, moment_two, update_sum = stepped(
                gradients[:, half * LANES : (half + 1) * LANES],
                weight_start,
                start_ref[j, COLS : 2 * COLS, :],
                start_ref[j, 2 * COLS : STATE, :],
                None,
            )
            states_ref[j, :COLS, :] = moment_one
            states_ref[j, COLS : 2 * COLS, :] = moment_two
            states_ref[j, 2 * COLS :, :] = update_sum
            weights.append((weight_start - learn_rate * update_sum).astype(BF16))
        part = turned_product(jnp.concatenate(weights, axis=1), table_ref[:, columns])
        total = part if total is None else total + part
    store_output(output_ref, total)


def first_step(gathered, error, start):
    vmem = pl.BlockSpec(memory_space=pltpu.VMEM)
    return pl.pallas_call(
        first_kernel,
        in_specs=[pl.BlockSpec(memory_space=pl.ANY), vmem, vmem],
        out_shape=[
            shaped(TABLE, SIDE * LANES, dtype=BF16),
            shaped(SIDE, STATE, LANES),
            shaped(SIDE, TILE, LANES),
        ],
        out_specs=[vmem, vmem, vmem],
        scratch_shapes=[
            pltpu.VMEM((SIDE, TABLE, LANES), F32),
            pltpu.SemaphoreType.DMA((SIDE,)),
        ],
        compiler_params=pltpu.CompilerParams(vmem_limit_bytes=20 * MIB),
    )(gathered, error, start)


def broadcast_error(output, constant_ref, step, out_ref):
    error = (output - constant_ref[STEPS]).astype(BF16).astype(F32)
    weighted = error * constant_ref[step]
    for j in range(SIDE):
        out_ref[j] = weighted


def first_error_kernel(parts_ref, constant_ref, out_ref):
    output = parts_ref[0, STATE:, :]
    for j in range(1, SIDE):
        output = output + parts_ref[j, STATE:, :]
    broadcast_error(output, constant_ref, 0, out_ref)


def error_kernel(step, parts_ref, constant_ref, out_ref):
    output = parts_ref[0]
    for j in range(1, SIDE):
        output = output + parts_ref[j]
    broadcast_error(output, constant_ref, step, out_ref)


def step_kernel(last, error_ref, table_ref, w_ref, states_ref, *rest):
    if last:
        (total_out,) = rest
    else:
        new_states, output_ref = rest
    both = whole_error(error_ref)
    weights = []
    for k in range(SIDE // 2):
        columns = slice(k * WIDE, (k + 1) * WIDE)
        product = jnp.dot(both, table_ref[:, columns], preferred_element_type=F32)
        gradients = (product[:COLS] + product[COLS:]) * (1.0 / TOKENS)
        for half in range(2):
            j = 2 * k + half
            weight_start = w_ref[j, :COLS, :]
            moment_one, moment_two, update_sum = stepped(
                gradients[:, half * LANES : (half + 1) * LANES],
                weight_start,
                states_ref[j, :COLS, :],
                states_ref[j, COLS : 2 * COLS, :],
                states_ref[j, 2 * COLS :, :],
            )
            if last:
                total_out[j] = update_sum
            else:
                new_states[j, :COLS, :] = moment_one
                new_states[j, COLS : 2 * COLS, :] = moment_two
                new_states[j, 2 * COLS :, :] = update_sum
                weights.append((weight_start - learn_rate * update_sum).astype(BF16))
    if last:
        return
    weights = jnp.concatenate(weights, axis=1)
    output = [
        turned_product(weights, table_ref[row : row + WIDE, :]) for row in range(0, TABLE, WIDE)
    ]
    store_output(output_ref, jnp.concatenate(output, axis=1))


def turn_kernel(parts_ref, out_ref):
    turned = parts_ref[...].reshape(SIDE * COLS, LANES).T
    out_ref[...] = turned.reshape(REPLICAS, LANES // REPLICAS, SIDE * COLS)


def gram_kernel(updates_ref, out_ref):
    updates = [updates_ref[r] for r in range(REPLICAS)]
    lines = []
    for i, j in PAIRS:
        product = updates[i] * updates[j]
        lines.append(jnp.sum(product, axis=0, keepdims=True))
    while len(lines) % 8:
        lines.append(jnp.zeros_like(lines[0]))
    sums = jnp.sum(jnp.concatenate(lines, axis=0), axis=1, keepdims=True)
    spread = jnp.broadcast_to(sums, (len(lines), LANES))
    line = lax.broadcasted_iota(jnp.int32, spread.shape, 0)
    lane = lax.broadcasted_iota(jnp.int32, spread.shape, 1)
    packed = jnp.sum(jnp.where(line == lane, spread, 0.0), axis=0, keepdims=True)
    for j in range(REPLICAS):
        out_ref[j] = packed


def gram_sum_kernel(parts_ref, out_ref):
    packed = jnp.sum(parts_ref[...], axis=0)
    for j in range(SIDE * SIDE):
        out_ref[j] = packed


def merge_kernel(parts_ref, updates_ref, out_ref):
    packed = jnp.sum(parts_ref[...], axis=0)
    lane = lax.broadcasted_iota(jnp.int32, packed.shape, 1)
    gram = {}
    for place, (i, j) in enumerate(PAIRS):
        value = jnp.sum(jnp.where(lane == place, packed, 0.0), axis=1, keepdims=True)
        gram[i, j] = value
        gram[j, i] = value
    members = [[r] for r in range(REPLICAS)]
    while len(members) > 1:
        merged = []
        for lower, upper in zip(members[0::2], members[1::2]):
            cross_dot = sum(gram[i, j] for i in lower for j in upper)
            lower_norm = sum(gram[i, j] for i in lower for j in lower)
            upper_norm = sum(gram[i, j] for i in upper for j in upper)
            lower_coef = 1.0 - cross_dot / (2.0 * (lower_norm + norm_eps))
            upper_coef = 1.0 - cross_dot / (2.0 * (upper_norm + norm_eps))
            scale = {**{i: lower_coef for i in lower}, **{i: upper_coef for i in upper}}
            merged.append((lower + upper, scale))
        factor = {i: scale[i] for _, scale in merged for i in scale}
        gram = {(i, j): factor[i] * factor[j] * value for (i, j), value in gram.items()}
        total = factor if len(merged) * 2 == REPLICAS else {i: total[i] * factor[i] for i in total}
        members = [group for group, _ in merged]
    result = total[0] * updates_ref[0]
    for r in range(1, REPLICAS):
        result = result + total[r] * updates_ref[r]
    out_ref[...] = result


def on_device(
    weight,
    first_moment,
    second_moment,
    token_ids,
    shared_inputs,
    private_inputs,
    shared_targets,
    private_targets,
):
    core = lax.axis_index("core")
    z = lax.axis_index("z")
    y = lax.axis_index("y")
    sum_place = jnp.where(core == 0, z, y)
    gather_place = jnp.where(core == 0, y, z)

    places = jnp.stack([sum_place, gather_place]).astype(jnp.int32)

    own = kernel_call(widen_kernel, shaped(TABLE, LANES), shared_inputs, private_inputs[0])
    gathered = lax.all_gather(
        own, CZY, axis=0, tiled=True, axis_index_groups=GATHER_GROUPS
    ).reshape(SIDE, TABLE, LANES)

    parts = kernel_call(own_kernel, shaped(SIDE, SIDE * TILE, LANES), own, weight)
    parts = exchange(parts, CZY, SUM_GROUPS)
    constants = own_constants(places, token_ids[0], shared_targets, private_targets[0])
    start = kernel_call(
        between_kernel,
        shaped(SIDE, STATE + TILE, LANES),
        parts,
        weight,
        first_moment[0],
        second_moment[0],
    )
    start = exchange(start, CZY, GATHER_GROUPS)
    error = kernel_call(first_error_kernel, shaped(SIDE, TILE, LANES), start, constants)
    error = exchange(error, CZY, SUM_GROUPS)
    table, states, parts = first_step(gathered, error, start)

    for step in range(1, STEPS):
        parts = exchange(parts, CZY, SUM_GROUPS)
        error = kernel_call(
            functools.partial(error_kernel, step), shaped(SIDE, TILE, LANES), parts, constants
        )
        error = exchange(error, CZY, SUM_GROUPS)
        last = step == STEPS - 1
        body = functools.partial(step_kernel, last)
        operands = (error, table, start, states)
        if last:
            updates = kernel_call(body, shaped(SIDE, COLS, LANES), *operands)
        else:
            states, parts = kernel_call(
                body, [shaped(SIDE, STATE, LANES), shaped(SIDE, TILE, LANES)], *operands
            )

    updates = exchange(updates, CZY, GATHER_GROUPS)
    turned = kernel_call(turn_kernel, shaped(REPLICAS, LANES // REPLICAS, SIDE * COLS), updates)
    updates = exchange(turned, ("x", "core"))
    gram = kernel_call(gram_kernel, shaped(REPLICAS, 1, LANES), updates)
    gram = exchange(gram, ("x", "core"))
    gram = kernel_call(gram_sum_kernel, shaped(SIDE * SIDE, 1, LANES), gram)
    gram = exchange(gram, ("z", "y"))
    return kernel_call(
        merge_kernel, shaped(LANES // REPLICAS, SIDE * COLS), gram, updates
    )


def solution(mesh):
    torus = Mesh(mesh.devices.reshape(4, 2, SIDE, SIDE), ("x", "core", "z", "y"))
    row = ("z", "y")
    rep = ("x", "core")
    placed = (
        P(row, None),
        P(rep, row, None),
        P(rep, row, None),
        P(rep, None, None),
        P(None, row),
        P(rep, None, row),
        P(),
        P(rep, None, None),
    )
    return jax.shard_map(
        on_device,
        mesh=torus,
        in_specs=placed,
        out_specs=P((*row, *rep), None),
        check_vma=False,
    )
```

```python
import functools

import jax
import jax.numpy as jnp
from jax import lax
from jax.experimental import pallas as pl
from jax.experimental.pallas import tpu as pltpu
from jax.sharding import Mesh
from jax.sharding import PartitionSpec as P

CZY = ("core", "z", "y")
F32 = jnp.float32
BF16 = jnp.bfloat16

learn_rate = 0.001
beta_one = 0.9
beta_two = 0.95
adam_eps = 1e-08
weight_decay = 0.1
norm_eps = 1e-06

SIDE = 8
LANES = 128
COLS = 48
HALF = COLS // 2
OWN = COLS // SIDE
FIRST = HALF + 2 * SIDE
CHIPS = 4
STATE = 3 * COLS
TILE = COLS + HALF
POOL = 1024
TABLE = 1536
STEPS = 4
TOKENS = 1024
REPLICAS = 8
PAIRS = [(i, j) for i in range(REPLICAS) for j in range(i, REPLICAS)]
MIB = 1024 * 1024
WIDE = 2 * LANES


def position(core, z, y):
    return (core * SIDE + z) * SIDE + y


SUM_GROUPS = [[position(0, z, y) for z in range(SIDE)] for y in range(SIDE)] + [
    [position(1, z, y) for y in range(SIDE)] for z in range(SIDE)
]
GATHER_GROUPS = [[position(0, z, y) for y in range(SIDE)] for z in range(SIDE)] + [
    [position(1, z, y) for z in range(SIDE)] for y in range(SIDE)
]


def exchange(blocks, axes, groups=None):
    return lax.all_to_all(
        blocks, axes, split_axis=0, concat_axis=0, tiled=True, axis_index_groups=groups
    )


def kernel_call(body, out_shapes, *operands, room=12):
    in_specs = [
        pl.BlockSpec(memory_space=pltpu.SMEM if operand.dtype == jnp.int32 else pltpu.VMEM)
        for operand in operands
    ]
    return pl.pallas_call(
        body,
        in_specs=in_specs,
        out_shape=out_shapes,
        compiler_params=pltpu.CompilerParams(vmem_limit_bytes=room * MIB),
    )(*operands)


def shaped(*dims, dtype=F32):
    return jax.ShapeDtypeStruct(dims, dtype)


def store_output(out_ref, output):
    for j in range(SIDE):
        out_ref[j, :COLS, :] = output[:, j * LANES : (j + 1) * LANES]
        private = POOL + (j // 2) * LANES
        line = (j % 2) * HALF
        out_ref[j, COLS:, :] = output[line : line + HALF, private : private + LANES]


def turned_product(left, right):
    return lax.dot_general(left, right, (((1,), (1,)), ((), ())), preferred_element_type=F32)


def in_two_parts(error):
    high = error.astype(BF16)
    low = (error - high.astype(F32)).astype(BF16)
    return jnp.concatenate([high, low], axis=0)


def whole_error(error_ref):
    error = jnp.concatenate(
        [error_ref[j, :COLS, :] for j in range(SIDE)]
        + [
            jnp.concatenate([error_ref[2 * k, COLS:, :], error_ref[2 * k + 1, COLS:, :]], axis=0)
            for k in range(SIDE // 2)
        ],
        axis=1,
    )
    return in_two_parts(error)


def stepped(gradient, weight_start, moment_one, moment_two, update_sum):
    if update_sum is None:
        weight_now = weight_start
    else:
        weight_now = weight_start - learn_rate * update_sum
    moment_one = beta_one * moment_one + (1.0 - beta_one) * gradient
    moment_two = beta_two * moment_two + (1.0 - beta_two) * gradient * gradient
    direction = moment_one / (jnp.sqrt(moment_two) + adam_eps) + weight_decay * weight_now
    update_sum = direction if update_sum is None else update_sum + direction
    return moment_one, moment_two, update_sum


def widen_kernel(shared_ref, private_ref, out_ref):
    out_ref[:POOL, :] = shared_ref[...].astype(F32)
    out_ref[POOL:, :] = private_ref[...].astype(F32)


def own_kernel(place_ref, slice_ref, weight_ref, constant_ref, out_ref):
    weights = weight_ref[...].astype(F32).T.astype(BF16)
    line = lax.broadcasted_iota(jnp.int32, (SIDE * SIDE * SIDE, SIDE * COLS), 0)
    lane = lax.broadcasted_iota(jnp.int32, (SIDE * SIDE * SIDE, SIDE * COLS), 1)
    spot = line & (SIDE - 1)
    column = ((line >> 3) & (SIDE - 1)) * COLS + (line >> 6) * OWN + spot
    order = jnp.where((lane == column) & (spot < OWN), 1.0, 0.0).astype(BF16)
    ordered = jnp.dot(order, weights, preferred_element_type=F32).astype(BF16)
    quarter = pl.ds(pl.multiple_of(place_ref[2] * WIDE, WIDE), WIDE)
    shared = turned_product(ordered, slice_ref[quarter, :].astype(BF16))
    for i in range(SIDE):
        for j in range(SIDE):
            line = (i * SIDE + j) * SIDE
            place = j * FIRST + HALF
            out_ref[i, place : place + SIDE, :] = shared[line : line + SIDE, :LANES]
            out_ref[i, place + SIDE : place + 2 * SIDE, :] = shared[line : line + SIDE, LANES:]
    for k in range(SIDE // 2):
        row = POOL + k * LANES
        private = turned_product(weights, slice_ref[row : row + LANES, :].astype(BF16))
        for j in range(SIDE):
            for half in range(2):
                line = j * COLS + half * HALF
                place = j * FIRST
                out_ref[2 * k + half, place : place + HALF, :] = private[line : line + HALF, :]


def constant_kernel(
    place_ref, ids_ref, shared_ref, private_ref, out_ref, first_ref, row_ref, rows, turned, arrived
):
    i, j, x = place_ref[0], place_ref[1], place_ref[2]
    shared_rows = pl.ds(pl.multiple_of(i * LANES, LANES), LANES)
    private_rows = pl.ds(pl.multiple_of(lax.div(i, 2) * LANES, LANES), LANES)
    quarter = pl.ds(pl.multiple_of(x * WIDE, WIDE), WIDE)
    copies = [
        pltpu.make_async_copy(shared_ref.at[shared_rows], rows.at[pl.ds(0, LANES)], arrived.at[0]),
        pltpu.make_async_copy(
            private_ref.at[private_rows], rows.at[pl.ds(LANES, LANES)], arrived.at[1]
        ),
        pltpu.make_async_copy(shared_ref.at[quarter], rows.at[pl.ds(WIDE, WIDE)], arrived.at[2]),
    ]
    for copy in copies:
        copy.start()
    row = lax.broadcasted_iota(jnp.int32, (LANES, TOKENS), 0)
    ones = jnp.ones((16, TOKENS), BF16)

    def count_of(step, start):
        hits = jnp.where(ids_ref[step : step + 1, :] == row + start, 1.0, 0.0).astype(BF16)
        return turned_product(ones, hits)

    for start in range(0, TABLE, LANES):
        row_ref[:, start : start + LANES] = count_of(0, start)[:SIDE]
    for start, lines in (
        (i * LANES, slice(0, COLS)),
        (POOL + lax.div(i, 2) * LANES, slice(COLS, TILE)),
    ):
        for step in range(1, STEPS):
            count = count_of(step, start)[:1]
            out_ref[step - 1, lines, :] = jnp.broadcast_to(
                count, (lines.stop - lines.start, LANES)
            )
    for copy in copies:
        copy.wait()
    turned[...] = rows[:LANES, :].astype(F32).T
    out_ref[STEPS - 1, :COLS, :] = turned[pl.ds(pl.multiple_of(j * COLS, 8), COLS), :]
    turned[...] = rows[LANES:WIDE, :].astype(F32).T
    columns = pl.ds(pl.multiple_of(j * COLS + lax.rem(i, 2) * HALF, 8), HALF)
    private = turned[columns, :]
    out_ref[STEPS - 1, COLS:, :] = private
    first_ref[:HALF, :] = private
    spot = lax.broadcasted_iota(jnp.int32, (16, SIDE * COLS), 0)
    lane = lax.broadcasted_iota(jnp.int32, (16, SIDE * COLS), 1)
    mine = (lane == j * COLS + i * OWN + spot) & (spot < OWN)
    shared = turned_product(jnp.where(mine, 1.0, 0.0).astype(BF16), rows[WIDE:, :])
    first_ref[HALF : HALF + SIDE, :] = shared[:SIDE, :LANES]
    first_ref[HALF + SIDE :, :] = shared[:SIDE, LANES:]


def own_constants(places, ids, shared_targets, private_targets):
    return pl.pallas_call(
        constant_kernel,
        in_specs=[
            pl.BlockSpec(memory_space=pltpu.SMEM),
            pl.BlockSpec(memory_space=pltpu.VMEM),
            pl.BlockSpec(memory_space=pl.ANY),
            pl.BlockSpec(memory_space=pl.ANY),
        ],
        out_shape=[shaped(STEPS, TILE, LANES), shaped(FIRST, LANES), shaped(SIDE, TABLE)],
        scratch_shapes=[
            pltpu.VMEM((2 * WIDE, SIDE * COLS), BF16),
            pltpu.VMEM((SIDE * COLS, LANES), F32),
            pltpu.SemaphoreType.DMA((3,)),
        ],
        compiler_params=pltpu.CompilerParams(vmem_limit_bytes=8 * MIB),
    )(places, ids, shared_targets, private_targets)


def between_kernel(parts_ref, w_ref, m_ref, v_ref, out_ref):
    for part, ref in enumerate((w_ref, m_ref, v_ref)):
        turned = ref[...].astype(F32).T.reshape(SIDE, COLS, LANES)
        out_ref[:, part * COLS : (part + 1) * COLS, :] = turned
    for j in range(SIDE):
        lines = slice(j * FIRST, (j + 1) * FIRST)
        output = parts_ref[0, lines, :]
        for source in range(1, SIDE):
            output = output + parts_ref[source, lines, :]
        out_ref[j, STATE:, :] = output


def first_whole_error(error_ref, row_ref):
    private = jnp.concatenate(
        [
            jnp.concatenate([error_ref[2 * k, :HALF, :], error_ref[2 * k + 1, :HALF, :]], axis=0)
            for k in range(SIDE // 2)
        ],
        axis=1,
    )
    padded = jnp.concatenate(
        [
            jnp.concatenate(
                [error_ref[i, HALF + b * SIDE : HALF + (b + 1) * SIDE, :] for i in range(SIDE)],
                axis=0,
            )
            for b in range(SIDE)
        ],
        axis=1,
    ).astype(BF16)
    line = lax.broadcasted_iota(jnp.int32, (COLS, SIDE * SIDE), 0)
    lane = lax.broadcasted_iota(jnp.int32, (COLS, SIDE * SIDE), 1)
    spot = lane & (SIDE - 1)
    kept = (line == (lane >> 3) * OWN + spot) & (spot < OWN)
    shared = jnp.dot(
        jnp.where(kept, 1.0, 0.0).astype(BF16), padded, preferred_element_type=F32
    )
    error = jnp.concatenate([shared, private], axis=1) * row_ref[:1, :]
    return in_two_parts(error)


def first_kernel(
    gathered_ref, error_ref, row_ref, start_ref, table_ref, states_ref, output_ref, slices, arrived
):
    copies = [
        pltpu.make_async_copy(gathered_ref.at[j], slices.at[j], arrived.at[j]) for j in range(SIDE)
    ]
    for copy in copies:
        copy.start()
    both = first_whole_error(error_ref, row_ref)
    total = None
    for k in range(SIDE // 2):
        copies[2 * k].wait()
        copies[2 * k + 1].wait()
        pair = jnp.concatenate([slices[2 * k], slices[2 * k + 1]], axis=1).astype(BF16)
        columns = slice(k * WIDE, (k + 1) * WIDE)
        table_ref[:, columns] = pair
        product = jnp.dot(both, table_ref[:, columns], preferred_element_type=F32)
        gradients = (product[:COLS] + product[COLS:]) * (1.0 / TOKENS)
        weights = []
        for half in range(2):
            j = 2 * k + half
            weight_start = start_ref[j, :COLS, :]
            moment_one, moment_two, update_sum = stepped(
                gradients[:, half * LANES : (half + 1) * LANES],
                weight_start,
                start_ref[j, COLS : 2 * COLS, :],
                start_ref[j, 2 * COLS : STATE, :],
                None,
            )
            states_ref[j, :COLS, :] = moment_one
            states_ref[j, COLS : 2 * COLS, :] = moment_two
            states_ref[j, 2 * COLS :, :] = update_sum
            weights.append((weight_start - learn_rate * update_sum).astype(BF16))
        part = turned_product(jnp.concatenate(weights, axis=1), table_ref[:, columns])
        total = part if total is None else total + part
    store_output(output_ref, total)


def first_step(gathered, error, count_row, start):
    vmem = pl.BlockSpec(memory_space=pltpu.VMEM)
    return pl.pallas_call(
        first_kernel,
        in_specs=[pl.BlockSpec(memory_space=pl.ANY), vmem, vmem, vmem],
        out_shape=[
            shaped(TABLE, SIDE * LANES, dtype=BF16),
            shaped(SIDE, STATE, LANES),
            shaped(SIDE, TILE, LANES),
        ],
        out_specs=[vmem, vmem, vmem],
        scratch_shapes=[
            pltpu.VMEM((SIDE, TABLE, LANES), F32),
            pltpu.SemaphoreType.DMA((SIDE,)),
        ],
        compiler_params=pltpu.CompilerParams(vmem_limit_bytes=44 * MIB),
    )(gathered, error, count_row, start)


def first_error_kernel(parts_ref, target_ref, private_ref, shared_ref):
    output = parts_ref[0, STATE:, :]
    for j in range(1, SIDE):
        output = output + parts_ref[j, STATE:, :]
    error = (output - target_ref[...]).astype(BF16).astype(F32)
    private_ref[...] = error[:HALF]
    for x in range(CHIPS):
        shared_ref[x] = error[HALF:]


def collect_kernel(private_ref, shared_ref, out_ref):
    for j in range(SIDE):
        out_ref[j, :HALF, :] = private_ref[...]
        for x in range(CHIPS):
            line = HALF + 2 * SIDE * x
            out_ref[j, line : line + 2 * SIDE, :] = shared_ref[x]


def error_kernel(step, parts_ref, constant_ref, out_ref):
    output = parts_ref[0]
    for j in range(1, SIDE):
        output = output + parts_ref[j]
    error = (output - constant_ref[STEPS - 1]).astype(BF16).astype(F32)
    weighted = error * constant_ref[step - 1]
    for j in range(SIDE):
        out_ref[j] = weighted


def step_kernel(last, error_ref, table_ref, w_ref, states_ref, *rest):
    if last:
        (total_out,) = rest
    else:
        new_states, output_ref = rest
    both = whole_error(error_ref)
    weights = []
    for k in range(SIDE // 2):
        columns = slice(k * WIDE, (k + 1) * WIDE)
        product = jnp.dot(both, table_ref[:, columns], preferred_element_type=F32)
        gradients = (product[:COLS] + product[COLS:]) * (1.0 / TOKENS)
        for half in range(2):
            j = 2 * k + half
            weight_start = w_ref[j, :COLS, :]
            moment_one, moment_two, update_sum = stepped(
                gradients[:, half * LANES : (half + 1) * LANES],
                weight_start,
                states_ref[j, :COLS, :],
                states_ref[j, COLS : 2 * COLS, :],
                states_ref[j, 2 * COLS :, :],
            )
            if last:
                total_out[j] = update_sum
            else:
                new_states[j, :COLS, :] = moment_one
                new_states[j, COLS : 2 * COLS, :] = moment_two
                new_states[j, 2 * COLS :, :] = update_sum
                weights.append((weight_start - learn_rate * update_sum).astype(BF16))
    if last:
        return
    weights = jnp.concatenate(weights, axis=1)
    output = [
        turned_product(weights, table_ref[row : row + WIDE, :]) for row in range(0, TABLE, WIDE)
    ]
    store_output(output_ref, jnp.concatenate(output, axis=1))


def turn_kernel(parts_ref, out_ref):
    turned = parts_ref[...].reshape(SIDE * COLS, LANES).T
    out_ref[...] = turned.reshape(REPLICAS, LANES // REPLICAS, SIDE * COLS)


def gram_kernel(updates_ref, out_ref):
    updates = [updates_ref[r] for r in range(REPLICAS)]
    lines = []
    for i, j in PAIRS:
        product = updates[i] * updates[j]
        lines.append(jnp.sum(product, axis=0, keepdims=True))
    while len(lines) % 8:
        lines.append(jnp.zeros_like(lines[0]))
    sums = jnp.sum(jnp.concatenate(lines, axis=0), axis=1, keepdims=True)
    spread = jnp.broadcast_to(sums, (len(lines), LANES))
    line = lax.broadcasted_iota(jnp.int32, spread.shape, 0)
    lane = lax.broadcasted_iota(jnp.int32, spread.shape, 1)
    packed = jnp.sum(jnp.where(line == lane, spread, 0.0), axis=0, keepdims=True)
    for j in range(REPLICAS):
        out_ref[j] = packed


def gram_sum_kernel(parts_ref, out_ref):
    packed = jnp.sum(parts_ref[...], axis=0)
    for j in range(SIDE * SIDE):
        out_ref[j] = packed


def merge_kernel(parts_ref, updates_ref, out_ref):
    packed = jnp.sum(parts_ref[...], axis=0)
    lane = lax.broadcasted_iota(jnp.int32, packed.shape, 1)
    gram = {}
    for place, (i, j) in enumerate(PAIRS):
        value = jnp.sum(jnp.where(lane == place, packed, 0.0), axis=1, keepdims=True)
        gram[i, j] = value
        gram[j, i] = value
    members = [[r] for r in range(REPLICAS)]
    while len(members) > 1:
        merged = []
        for lower, upper in zip(members[0::2], members[1::2]):
            cross_dot = sum(gram[i, j] for i in lower for j in upper)
            lower_norm = sum(gram[i, j] for i in lower for j in lower)
            upper_norm = sum(gram[i, j] for i in upper for j in upper)
            lower_coef = 1.0 - cross_dot / (2.0 * (lower_norm + norm_eps))
            upper_coef = 1.0 - cross_dot / (2.0 * (upper_norm + norm_eps))
            scale = {**{i: lower_coef for i in lower}, **{i: upper_coef for i in upper}}
            merged.append((lower + upper, scale))
        factor = {i: scale[i] for _, scale in merged for i in scale}
        gram = {(i, j): factor[i] * factor[j] * value for (i, j), value in gram.items()}
        total = factor if len(merged) * 2 == REPLICAS else {i: total[i] * factor[i] for i in total}
        members = [group for group, _ in merged]
    result = total[0] * updates_ref[0]
    for r in range(1, REPLICAS):
        result = result + total[r] * updates_ref[r]
    out_ref[...] = result


def on_device(
    weight,
    first_moment,
    second_moment,
    token_ids,
    shared_inputs,
    private_inputs,
    shared_targets,
    private_targets,
):
    core = lax.axis_index("core")
    z = lax.axis_index("z")
    y = lax.axis_index("y")
    sum_place = jnp.where(core == 0, z, y)
    gather_place = jnp.where(core == 0, y, z)

    places = jnp.stack([sum_place, gather_place, lax.axis_index("x")]).astype(jnp.int32)

    own = kernel_call(widen_kernel, shaped(TABLE, LANES), shared_inputs, private_inputs[0])
    gathered = lax.all_gather(
        own, CZY, axis=0, tiled=True, axis_index_groups=GATHER_GROUPS
    ).reshape(SIDE, TABLE, LANES)

    constants, first_targets, count_row = own_constants(
        places, token_ids[0], shared_targets, private_targets[0]
    )
    parts = kernel_call(
        own_kernel, shaped(SIDE, SIDE * FIRST, LANES), places, own, weight, first_targets
    )
    parts = exchange(parts, CZY, SUM_GROUPS)
    start = kernel_call(
        between_kernel,
        shaped(SIDE, STATE + FIRST, LANES),
        parts,
        weight,
        first_moment[0],
        second_moment[0],
    )
    start = exchange(start, CZY, GATHER_GROUPS)
    private, shared = kernel_call(
        first_error_kernel,
        [shaped(HALF, LANES), shaped(CHIPS, 2 * SIDE, LANES)],
        start,
        first_targets,
    )
    shared = exchange(shared, "x")
    error = kernel_call(
        collect_kernel, shaped(SIDE, HALF + SIDE * SIDE, LANES), private, shared
    )
    error = exchange(error, CZY, SUM_GROUPS)
    table, states, parts = first_step(gathered, error, count_row, start)

    for step in range(1, STEPS):
        parts = exchange(parts, CZY, SUM_GROUPS)
        error = kernel_call(
            functools.partial(error_kernel, step), shaped(SIDE, TILE, LANES), parts, constants
        )
        error = exchange(error, CZY, SUM_GROUPS)
        last = step == STEPS - 1
        body = functools.partial(step_kernel, last)
        operands = (error, table, start, states)
        if last:
            updates = kernel_call(body, shaped(SIDE, COLS, LANES), *operands)
        else:
            states, parts = kernel_call(
                body, [shaped(SIDE, STATE, LANES), shaped(SIDE, TILE, LANES)], *operands
            )

    updates = exchange(updates, CZY, GATHER_GROUPS)
    turned = kernel_call(turn_kernel, shaped(REPLICAS, LANES // REPLICAS, SIDE * COLS), updates)
    updates = exchange(turned, ("x", "core"))
    gram = kernel_call(gram_kernel, shaped(REPLICAS, 1, LANES), updates)
    gram = exchange(gram, ("x", "core"))
    gram = kernel_call(gram_sum_kernel, shaped(SIDE * SIDE, 1, LANES), gram)
    gram = exchange(gram, ("z", "y"))
    return kernel_call(
        merge_kernel, shaped(LANES // REPLICAS, SIDE * COLS), gram, updates
    )


def solution(mesh):
    torus = Mesh(mesh.devices.reshape(4, 2, SIDE, SIDE), ("x", "core", "z", "y"))
    row = ("z", "y")
    rep = ("x", "core")
    placed = (
        P(row, None),
        P(rep, row, None),
        P(rep, row, None),
        P(rep, None, None),
        P(None, row),
        P(rep, None, row),
        P(),
        P(rep, None, None),
    )
    return jax.shard_map(
        on_device,
        mesh=torus,
        in_specs=placed,
        out_specs=P((*row, *rep), None),
        check_vma=False,
    )
```

```python
import functools

import jax
import jax.numpy as jnp
from jax import lax
from jax.experimental import pallas as pl
from jax.experimental.pallas import tpu as pltpu
from jax.sharding import Mesh
from jax.sharding import PartitionSpec as P

CZY = ("core", "z", "y")
F32 = jnp.float32
BF16 = jnp.bfloat16

learn_rate = 0.001
beta_one = 0.9
beta_two = 0.95
adam_eps = 1e-08
weight_decay = 0.1
norm_eps = 1e-06

SIDE = 8
LANES = 128
COLS = 48
HALF = COLS // 2
TILE = COLS + HALF
POOL = 1024
TABLE = 1536
STEPS = 4
TOKENS = 1024
REPLICAS = 8
PAIRS = [(i, j) for i in range(REPLICAS) for j in range(i, REPLICAS)]
MIB = 1024 * 1024
WIDE = 2 * LANES
OFFSETS = (0, 4, -1, 1, -2, 2, -3, 3)


def position(core, z, y):
    return (core * SIDE + z) * SIDE + y


SUM_GROUPS = [[position(0, z, y) for z in range(SIDE)] for y in range(SIDE)] + [
    [position(1, z, y) for y in range(SIDE)] for z in range(SIDE)
]
GATHER_GROUPS = [[position(0, z, y) for y in range(SIDE)] for z in range(SIDE)] + [
    [position(1, z, y) for z in range(SIDE)] for y in range(SIDE)
]


UP = [(group[i], group[(i + 1) % SIDE]) for group in GATHER_GROUPS for i in range(SIDE)]
DOWN = [(group[i], group[(i - 1) % SIDE]) for group in GATHER_GROUPS for i in range(SIDE)]


def exchange(blocks, axes, groups=None):
    return lax.all_to_all(
        blocks, axes, split_axis=0, concat_axis=0, tiled=True, axis_index_groups=groups
    )


def kernel_call(body, out_shapes, *operands, room=12):
    in_specs = [
        pl.BlockSpec(memory_space=pltpu.SMEM if operand.dtype == jnp.int32 else pltpu.VMEM)
        for operand in operands
    ]
    return pl.pallas_call(
        body,
        in_specs=in_specs,
        out_shape=out_shapes,
        compiler_params=pltpu.CompilerParams(vmem_limit_bytes=room * MIB),
    )(*operands)


def shaped(*dims, dtype=F32):
    return jax.ShapeDtypeStruct(dims, dtype)


def store_output(out_ref, output):
    for j in range(SIDE):
        out_ref[j, :COLS, :] = output[:, j * LANES : (j + 1) * LANES]
        private = POOL + (j // 2) * LANES
        line = (j % 2) * HALF
        out_ref[j, COLS:, :] = output[line : line + HALF, private : private + LANES]


def states_kernel(w_ref, m_ref, v_ref, out_ref):
    for part, ref in enumerate((w_ref, m_ref, v_ref)):
        turned = ref[...].astype(F32).T.reshape(SIDE, COLS, LANES)
        out_ref[:, part * COLS : (part + 1) * COLS, :] = turned


def widen_kernel(shared_ref, private_ref, out_ref, shared, private, arrived):
    copies = [
        pltpu.make_async_copy(shared_ref, shared, arrived.at[0]),
        pltpu.make_async_copy(private_ref, private, arrived.at[1]),
    ]
    for copy in copies:
        copy.start()
    copies[0].wait()
    out_ref[:POOL, :] = shared[...].astype(F32)
    copies[1].wait()
    out_ref[POOL:, :] = private[...].astype(F32)


def widened(shared_inputs, private_inputs):
    return pl.pallas_call(
        widen_kernel,
        in_specs=[pl.BlockSpec(memory_space=pltpu.HBM)] * 2,
        out_shape=shaped(TABLE, LANES),
        scratch_shapes=[
            pltpu.VMEM((POOL, LANES), BF16),
            pltpu.VMEM((TABLE - POOL, LANES), BF16),
            pltpu.SemaphoreType.DMA((2,)),
        ],
        compiler_params=pltpu.CompilerParams(vmem_limit_bytes=56 * MIB),
    )(shared_inputs, private_inputs)


def turned_product(left, right):
    return lax.dot_general(left, right, (((1,), (1,)), ((), ())), preferred_element_type=F32)


def constant_kernel(place_ref, ids_ref, shared_ref, private_ref, out_ref, rows, turned, arrived):
    i, j = place_ref[0], place_ref[1]
    shared_rows = pl.ds(pl.multiple_of(i * LANES, LANES), LANES)
    private_rows = pl.ds(pl.multiple_of(lax.div(i, 2) * LANES, LANES), LANES)
    copies = [
        pltpu.make_async_copy(shared_ref.at[shared_rows], rows.at[0], arrived.at[0]),
        pltpu.make_async_copy(private_ref.at[private_rows], rows.at[1], arrived.at[1]),
    ]
    for copy in copies:
        copy.start()
    row = lax.broadcasted_iota(jnp.int32, (LANES, TOKENS), 0)
    ones = jnp.ones((16, TOKENS), BF16)
    for start, lines in (
        (i * LANES, slice(0, COLS)),
        (POOL + lax.div(i, 2) * LANES, slice(COLS, TILE)),
    ):
        for step in range(STEPS):
            hits = jnp.where(ids_ref[step : step + 1, :] == row + start, 1.0, 0.0).astype(BF16)
            count = turned_product(ones, hits)[:1]
            out_ref[step, lines, :] = jnp.broadcast_to(count, (lines.stop - lines.start, LANES))
    for copy in copies:
        copy.wait()
    turned[...] = rows[0].astype(F32).T
    columns = pl.ds(pl.multiple_of(j * COLS, 8), COLS)
    out_ref[STEPS, :COLS, :] = turned[columns, :]
    turned[...] = rows[1].astype(F32).T
    columns = pl.ds(pl.multiple_of(j * COLS + lax.rem(i, 2) * HALF, 8), HALF)
    out_ref[STEPS, COLS:, :] = turned[columns, :]


def own_constants(places, ids, shared_targets, private_targets):
    return pl.pallas_call(
        constant_kernel,
        in_specs=[
            pl.BlockSpec(memory_space=pltpu.SMEM),
            pl.BlockSpec(memory_space=pltpu.VMEM),
            pl.BlockSpec(memory_space=pl.ANY),
            pl.BlockSpec(memory_space=pl.ANY),
        ],
        out_shape=shaped(STEPS + 1, TILE, LANES),
        scratch_shapes=[
            pltpu.VMEM((2, LANES, SIDE * COLS), BF16),
            pltpu.VMEM((SIDE * COLS, LANES), F32),
            pltpu.SemaphoreType.DMA((2,)),
        ],
        compiler_params=pltpu.CompilerParams(vmem_limit_bytes=8 * MIB),
    )(places, ids, shared_targets, private_targets)


def narrow_kernel(*refs):
    *blocks, out_ref, turned_ref = refs
    for k, block in enumerate(blocks):
        columns = slice(k * LANES, (k + 1) * LANES)
        narrow = block[...].astype(BF16)
        out_ref[:, columns] = narrow
        turned_ref[columns, :] = narrow.T


def narrowed(*blocks):
    columns = len(blocks) * LANES
    return kernel_call(
        narrow_kernel, [shaped(TABLE, columns, dtype=BF16), shaped(columns, TABLE, dtype=BF16)], *blocks
    )


def product_of(left, right):
    return jnp.dot(left, right, preferred_element_type=F32)


def weights_of(states_ref, *places):
    return jnp.concatenate([states_ref[k, :COLS, :] for k in places], axis=1).astype(BF16)


def early_kernel(place_ref, start_ref, constant_ref, own_ref, *refs):
    pairs, (states_ref, part_ref) = refs[:3], refs[3:]
    place = place_ref[1]
    for k, offset in enumerate(OFFSETS):
        states_ref[k] = start_ref[lax.rem(place + (offset + SIDE), SIDE)]
    part = product_of(weights_of(states_ref, 0), own_ref[...])
    for k, pair in enumerate(pairs):
        part = part + product_of(weights_of(states_ref, 2 * k + 2, 2 * k + 3), pair[...])
    part_ref[...] = part


def late_kernel(states_ref, opposite_ref, part_ref, table_ref, turned_ref, out_ref):
    narrow = opposite_ref[...].astype(BF16)
    table_ref[...] = narrow
    turned_ref[...] = narrow.T
    output = part_ref[...] + product_of(weights_of(states_ref, 1), turned_ref[...])
    store_output(out_ref, output)


def error_kernel(step, parts_ref, constant_ref, out_ref):
    output = parts_ref[0]
    for j in range(1, SIDE):
        output = output + parts_ref[j]
    error = (output - constant_ref[STEPS]).astype(BF16).astype(F32)
    weighted = error * constant_ref[step]
    for j in range(SIDE):
        out_ref[j] = weighted


def step_kernel(first, last, place_ref, error_ref, *refs):
    own, opposite, *pairs = refs[:5]
    if last:
        w_ref, states_ref, total_out = refs[5:]
        place = place_ref[1]
    else:
        turned, (w_ref, states_ref, new_states, output_ref) = refs[5:10], refs[10:]
    error = jnp.concatenate(
        [error_ref[j, :COLS, :] for j in range(SIDE)]
        + [
            jnp.concatenate([error_ref[2 * k, COLS:, :], error_ref[2 * k + 1, COLS:, :]], axis=0)
            for k in range(SIDE // 2)
        ],
        axis=1,
    )
    high = error.astype(BF16)
    low = (error - high.astype(F32)).astype(BF16)
    both = jnp.concatenate([high, low], axis=0)
    updated = []
    for k in range(SIDE // 2):
        if k == 0:
            columns = jnp.concatenate([own[...], opposite[...]], axis=1)
        else:
            columns = pairs[k - 1][...]
        product = product_of(both, columns)
        gradients = (product[:COLS] + product[COLS:]) * (1.0 / TOKENS)
        for half in range(2):
            j = 2 * k + half
            gradient = gradients[:, half * LANES : (half + 1) * LANES]
            weight_start = w_ref[j, :COLS, :]
            if first:
                weight_now = weight_start
            else:
                update_sum = states_ref[j, 2 * COLS :, :]
                weight_now = weight_start - learn_rate * update_sum
            base = COLS if first else 0
            moment_one = states_ref[j, base : base + COLS, :]
            moment_two = states_ref[j, base + COLS : base + 2 * COLS, :]
            moment_one = beta_one * moment_one + (1.0 - beta_one) * gradient
            moment_two = beta_two * moment_two + (1.0 - beta_two) * gradient * gradient
            direction = (
                moment_one / (jnp.sqrt(moment_two) + adam_eps) + weight_decay * weight_now
            )
            update_sum = direction if first else update_sum + direction
            if last:
                total_out[lax.rem(place + (OFFSETS[j] + SIDE), SIDE)] = update_sum
            else:
                new_states[j, :COLS, :] = moment_one
                new_states[j, COLS : 2 * COLS, :] = moment_two
                new_states[j, 2 * COLS :, :] = update_sum
                updated.append((weight_start - learn_rate * update_sum).astype(BF16))
    if last:
        return
    output = product_of(
        jnp.concatenate(updated[:2], axis=1),
        jnp.concatenate([turned[0][...], turned[1][...]], axis=0),
    )
    for k in range(1, SIDE // 2):
        weights = jnp.concatenate(updated[2 * k : 2 * k + 2], axis=1)
        output = output + product_of(weights, turned[k + 1][...])
    store_output(output_ref, output)


def turn_kernel(parts_ref, out_ref):
    turned = parts_ref[...].reshape(SIDE * COLS, LANES).T
    out_ref[...] = turned.reshape(REPLICAS, LANES // REPLICAS, SIDE * COLS)


def gram_kernel(updates_ref, out_ref):
    updates = [updates_ref[r] for r in range(REPLICAS)]
    lines = []
    for i, j in PAIRS:
        product = updates[i] * updates[j]
        lines.append(jnp.sum(product, axis=0, keepdims=True))
    while len(lines) % 8:
        lines.append(jnp.zeros_like(lines[0]))
    sums = jnp.sum(jnp.concatenate(lines, axis=0), axis=1, keepdims=True)
    spread = jnp.broadcast_to(sums, (len(lines), LANES))
    line = lax.broadcasted_iota(jnp.int32, spread.shape, 0)
    lane = lax.broadcasted_iota(jnp.int32, spread.shape, 1)
    packed = jnp.sum(jnp.where(line == lane, spread, 0.0), axis=0, keepdims=True)
    for j in range(REPLICAS):
        out_ref[j] = packed


def gram_sum_kernel(parts_ref, out_ref):
    packed = jnp.sum(parts_ref[...], axis=0)
    for j in range(SIDE * SIDE):
        out_ref[j] = packed


def merge_kernel(parts_ref, updates_ref, out_ref):
    packed = jnp.sum(parts_ref[...], axis=0)
    lane = lax.broadcasted_iota(jnp.int32, packed.shape, 1)
    gram = {}
    for place, (i, j) in enumerate(PAIRS):
        value = jnp.sum(jnp.where(lane == place, packed, 0.0), axis=1, keepdims=True)
        gram[i, j] = value
        gram[j, i] = value
    members = [[r] for r in range(REPLICAS)]
    while len(members) > 1:
        merged = []
        for lower, upper in zip(members[0::2], members[1::2]):
            cross_dot = sum(gram[i, j] for i in lower for j in upper)
            lower_norm = sum(gram[i, j] for i in lower for j in lower)
            upper_norm = sum(gram[i, j] for i in upper for j in upper)
            lower_coef = 1.0 - cross_dot / (2.0 * (lower_norm + norm_eps))
            upper_coef = 1.0 - cross_dot / (2.0 * (upper_norm + norm_eps))
            scale = {**{i: lower_coef for i in lower}, **{i: upper_coef for i in upper}}
            merged.append((lower + upper, scale))
        factor = {i: scale[i] for _, scale in merged for i in scale}
        gram = {(i, j): factor[i] * factor[j] * value for (i, j), value in gram.items()}
        total = factor if len(merged) * 2 == REPLICAS else {i: total[i] * factor[i] for i in total}
        members = [group for group, _ in merged]
    result = total[0] * updates_ref[0]
    for r in range(1, REPLICAS):
        result = result + total[r] * updates_ref[r]
    out_ref[...] = result


def on_device(
    weight,
    first_moment,
    second_moment,
    token_ids,
    shared_inputs,
    private_inputs,
    shared_targets,
    private_targets,
):
    core = lax.axis_index("core")
    z = lax.axis_index("z")
    y = lax.axis_index("y")
    sum_place = jnp.where(core == 0, z, y)
    gather_place = jnp.where(core == 0, y, z)

    places = jnp.stack([sum_place, gather_place]).astype(jnp.int32)
    constants = own_constants(places, token_ids[0], shared_targets, private_targets[0])
    own = widened(shared_inputs, private_inputs[0])
    own_table, own_turned = narrowed(own)
    tables = []
    upward = downward = own
    for hop in range(3):
        if hop >= 2:
            upward, tables[hop - 2] = lax.optimization_barrier((upward, tables[hop - 2]))
        upward = lax.ppermute(upward, CZY, UP)
        downward = lax.ppermute(downward, CZY, DOWN)
        tables.append(narrowed(upward, downward))
    opposite, tables[1] = lax.optimization_barrier((upward, tables[1]))
    opposite = lax.ppermute(opposite, CZY, UP)

    start = kernel_call(
        states_kernel, shaped(SIDE, 3 * COLS, LANES), weight, first_moment[0], second_moment[0]
    )
    start = exchange(start, CZY, GATHER_GROUPS)
    start, part = kernel_call(
        early_kernel,
        [shaped(SIDE, 3 * COLS, LANES), shaped(COLS, TABLE)],
        places,
        start,
        constants,
        own_turned,
        *[turned for _, turned in tables],
        room=20,
    )
    opposite_table, opposite_turned, parts = kernel_call(
        late_kernel,
        [
            shaped(TABLE, LANES, dtype=BF16),
            shaped(LANES, TABLE, dtype=BF16),
            shaped(SIDE, TILE, LANES),
        ],
        start,
        opposite,
        part,
    )
    tables = [(own_table, own_turned), (opposite_table, opposite_turned), *tables]
    states = start
    for step in range(STEPS):
        parts = exchange(parts, CZY, SUM_GROUPS)
        error = kernel_call(
            functools.partial(error_kernel, step), shaped(SIDE, TILE, LANES), parts, constants
        )
        error = exchange(error, CZY, SUM_GROUPS)
        last = step == STEPS - 1
        body = functools.partial(step_kernel, step == 0, last)
        operands = (places, error, *[table for table, _ in tables])
        if last:
            updates = kernel_call(body, shaped(SIDE, COLS, LANES), *operands, start, states)
        else:
            states, parts = kernel_call(
                body,
                [shaped(SIDE, 3 * COLS, LANES), shaped(SIDE, TILE, LANES)],
                *operands,
                *[turned for _, turned in tables],
                start,
                states,
            )

    updates = exchange(updates, CZY, GATHER_GROUPS)
    turned = kernel_call(turn_kernel, shaped(REPLICAS, LANES // REPLICAS, SIDE * COLS), updates)
    updates = exchange(turned, ("x", "core"))
    gram = kernel_call(gram_kernel, shaped(REPLICAS, 1, LANES), updates)
    gram = exchange(gram, ("x", "core"))
    gram = kernel_call(gram_sum_kernel, shaped(SIDE * SIDE, 1, LANES), gram)
    gram = exchange(gram, ("z", "y"))
    return kernel_call(
        merge_kernel, shaped(LANES // REPLICAS, SIDE * COLS), gram, updates
    )


def solution(mesh):
    torus = Mesh(mesh.devices.reshape(4, 2, SIDE, SIDE), ("x", "core", "z", "y"))
    row = ("z", "y")
    rep = ("x", "core")
    placed = (
        P(row, None),
        P(rep, row, None),
        P(rep, row, None),
        P(rep, None, None),
        P(None, row),
        P(rep, None, row),
        P(),
        P(rep, None, None),
    )
    return jax.shard_map(
        on_device,
        mesh=torus,
        in_specs=placed,
        out_specs=P((*row, *rep), None),
        check_vma=False,
    )
```

```python
import functools

import jax
import jax.numpy as jnp
from jax import lax
from jax.experimental import pallas as pl
from jax.experimental.pallas import tpu as pltpu
from jax.sharding import Mesh
from jax.sharding import PartitionSpec as P

CZY = ("core", "z", "y")
F32 = jnp.float32
BF16 = jnp.bfloat16

learn_rate = 0.001
beta_one = 0.9
beta_two = 0.95
adam_eps = 1e-08
weight_decay = 0.1
norm_eps = 1e-06

SIDE = 8
LANES = 128
COLS = 48
POOL = 1024
TABLE = 1536
STEPS = 4
TOKENS = 1024
REPLICAS = 8
PAIRS = [(i, j) for i in range(REPLICAS) for j in range(i, REPLICAS)]
MIB = 1024 * 1024
WIDE = 2 * LANES
OFFSETS = (0, -1, 1, -2, 2, -3, 3, 4)


def position(core, z, y):
    return (core * SIDE + z) * SIDE + y


SUM_GROUPS = [[position(0, z, y) for z in range(SIDE)] for y in range(SIDE)] + [
    [position(1, z, y) for y in range(SIDE)] for z in range(SIDE)
]
GATHER_GROUPS = [[position(0, z, y) for y in range(SIDE)] for z in range(SIDE)] + [
    [position(1, z, y) for z in range(SIDE)] for y in range(SIDE)
]


UP = [(group[i], group[(i + 1) % SIDE]) for group in GATHER_GROUPS for i in range(SIDE)]
DOWN = [(group[i], group[(i - 1) % SIDE]) for group in GATHER_GROUPS for i in range(SIDE)]


def exchange(blocks, axes, groups=None):
    return lax.all_to_all(
        blocks, axes, split_axis=0, concat_axis=0, tiled=True, axis_index_groups=groups
    )


def kernel_call(body, out_shapes, *operands, room=12):
    in_specs = [
        pl.BlockSpec(memory_space=pltpu.SMEM if operand.dtype == jnp.int32 else pltpu.VMEM)
        for operand in operands
    ]
    return pl.pallas_call(
        body,
        in_specs=in_specs,
        out_shape=out_shapes,
        compiler_params=pltpu.CompilerParams(vmem_limit_bytes=room * MIB),
    )(*operands)


def shaped(*dims, dtype=F32):
    return jax.ShapeDtypeStruct(dims, dtype)


def product_of(left, right):
    return jnp.dot(left, right, preferred_element_type=F32)


def turned_product(left, right):
    return lax.dot_general(left, right, (((1,), (1,)), ((), ())), preferred_element_type=F32)


def store_output(out_ref, token, output):
    for half in range(2):
        out_ref[token // LANES + half] = output[:, half * LANES : (half + 1) * LANES]


def states_kernel(w_ref, m_ref, v_ref, out_ref):
    for part, ref in enumerate((w_ref, m_ref, v_ref)):
        turned = ref[...].astype(F32).T.reshape(SIDE, COLS, LANES)
        out_ref[:, part * COLS : (part + 1) * COLS, :] = turned


def widen_kernel(shared_ref, private_ref, out_ref, shared, private, arrived):
    copies = [
        pltpu.make_async_copy(shared_ref, shared, arrived.at[0]),
        pltpu.make_async_copy(private_ref, private, arrived.at[1]),
    ]
    for copy in copies:
        copy.start()
    copies[0].wait()
    out_ref[:POOL, :] = shared[...].astype(F32)
    copies[1].wait()
    out_ref[POOL:, :] = private[...].astype(F32)


def widened(shared_inputs, private_inputs):
    return pl.pallas_call(
        widen_kernel,
        in_specs=[pl.BlockSpec(memory_space=pltpu.HBM)] * 2,
        out_shape=shaped(TABLE, LANES),
        scratch_shapes=[
            pltpu.VMEM((POOL, LANES), BF16),
            pltpu.VMEM((TABLE - POOL, LANES), BF16),
            pltpu.SemaphoreType.DMA((2,)),
        ],
        compiler_params=pltpu.CompilerParams(vmem_limit_bytes=4 * MIB),
    )(shared_inputs, private_inputs)


def choice(ids, width=TABLE, start=0):
    row = lax.broadcasted_iota(jnp.int32, (ids.shape[0], width), 1).astype(F32) + start
    return jnp.where(row == ids, 1.0, 0.0).astype(BF16)


def choose(ids_ref, step, pair, out_ref):
    for token in range(0, TOKENS, WIDE):
        tokens = slice(token, token + WIDE)
        chosen = choice(ids_ref[tokens, step : step + 1])
        out_ref[tokens, :] = product_of(chosen, pair).astype(BF16)


def target_kernel(place_ref, ids_ref, shared_ref, private_ref, target_ref, turned):
    own = pl.ds(pl.multiple_of(place_ref[0] * LANES, LANES), LANES)
    columns = pl.ds(pl.multiple_of(place_ref[1] * COLS, 16), COLS)
    for step in range(STEPS):
        ids = ids_ref[own, step : step + 1]
        targets = product_of(choice(ids, POOL), shared_ref[...])
        targets = targets + product_of(choice(ids, TABLE - POOL, POOL), private_ref[...])
        turned[...] = targets.T
        target_ref[step] = turned[columns, :]


def own_targets(places, ids, shared_targets, private_targets):
    return pl.pallas_call(
        target_kernel,
        in_specs=[pl.BlockSpec(memory_space=pltpu.SMEM)]
        + [pl.BlockSpec(memory_space=pltpu.VMEM)] * 3,
        out_shape=shaped(STEPS, COLS, LANES),
        scratch_shapes=[pltpu.VMEM((SIDE * COLS, LANES), F32)],
        compiler_params=pltpu.CompilerParams(vmem_limit_bytes=12 * MIB),
    )(places, ids, shared_targets, private_targets)


def pair_of(first_ref, second_ref):
    return jnp.concatenate([first_ref[...], second_ref[...]], axis=1).astype(BF16)


def rows_kernel(ids_ref, first_ref, second_ref, *outs):
    pair = pair_of(first_ref, second_ref)
    for step in range(STEPS):
        choose(ids_ref, step, pair, outs[step])


def chosen_rows(ids, first, second):
    return kernel_call(
        rows_kernel, [shaped(TOKENS, WIDE, dtype=BF16)] * STEPS, ids, first, second
    )


def early_kernel(place_ref, start_ref, target_ref, *refs):
    pairs, (states_ref, part_ref) = refs[:3], refs[3:]
    place = place_ref[1]
    for k, offset in enumerate(OFFSETS):
        states_ref[k] = start_ref[lax.rem(place + (offset + SIDE), SIDE)]
    weights = jnp.concatenate([states_ref[k, :COLS, :] for k in range(6)], axis=1).astype(BF16)
    for token in range(0, TOKENS, WIDE):
        tokens = slice(token, token + WIDE)
        rows = jnp.concatenate([pair[tokens, :] for pair in pairs], axis=1)
        part_ref[:, tokens] = turned_product(weights, rows)


def late_kernel(ids_ref, states_ref, first_ref, second_ref, part_ref, *outs):
    out_ref = outs[STEPS]
    pair = pair_of(first_ref, second_ref)
    weights = jnp.concatenate([states_ref[k, :COLS, :] for k in (6, 7)], axis=1).astype(BF16)
    for step in range(STEPS):
        choose(ids_ref, step, pair, outs[step])
    for token in range(0, TOKENS, WIDE):
        tokens = slice(token, token + WIDE)
        output = part_ref[:, tokens] + turned_product(weights, outs[0][tokens, :])
        store_output(out_ref, token, output)


def error_kernel(step, parts_ref, target_ref, out_ref):
    output = parts_ref[0]
    for j in range(1, SIDE):
        output = output + parts_ref[j]
    error = (output - target_ref[step]).astype(BF16).astype(F32)
    for j in range(SIDE):
        out_ref[j] = error


def step_kernel(first, last, place_ref, error_ref, w_ref, states_ref, *refs):
    pairs, rest = refs[: SIDE // 2], refs[SIDE // 2 :]
    if last:
        (total_out,) = rest
        place = place_ref[1]
    else:
        next_pairs, (new_states, output_ref) = rest[: SIDE // 2], rest[SIDE // 2 :]
    error = jnp.concatenate([error_ref[j] for j in range(SIDE)], axis=1).astype(BF16)
    updated = []
    for k in range(SIDE // 2):
        gradients = product_of(error, pairs[k][...]) * (1.0 / TOKENS)
        for half in range(2):
            j = 2 * k + half
            gradient = gradients[:, half * LANES : (half + 1) * LANES]
            weight_start = w_ref[j, :COLS, :]
            if first:
                weight_now = weight_start
            else:
                update_sum = states_ref[j, 2 * COLS :, :]
                weight_now = weight_start - learn_rate * update_sum
            base = COLS if first else 0
            moment_one = states_ref[j, base : base + COLS, :]
            moment_two = states_ref[j, base + COLS : base + 2 * COLS, :]
            moment_one = beta_one * moment_one + (1.0 - beta_one) * gradient
            moment_two = beta_two * moment_two + (1.0 - beta_two) * gradient * gradient
            direction = (
                moment_one / (jnp.sqrt(moment_two) + adam_eps) + weight_decay * weight_now
            )
            update_sum = direction if first else update_sum + direction
            if last:
                total_out[lax.rem(place + (OFFSETS[j] + SIDE), SIDE)] = update_sum
            else:
                new_states[j, :COLS, :] = moment_one
                new_states[j, COLS : 2 * COLS, :] = moment_two
                new_states[j, 2 * COLS :, :] = update_sum
                updated.append((weight_start - learn_rate * update_sum).astype(BF16))
    if last:
        return
    weights = jnp.concatenate(updated, axis=1)
    for token in range(0, TOKENS, WIDE):
        tokens = slice(token, token + WIDE)
        rows = jnp.concatenate([pair[tokens, :] for pair in next_pairs], axis=1)
        store_output(output_ref, token, turned_product(weights, rows))


def turn_kernel(parts_ref, out_ref):
    turned = parts_ref[...].reshape(SIDE * COLS, LANES).T
    out_ref[...] = turned.reshape(REPLICAS, LANES // REPLICAS, SIDE * COLS)


def gram_kernel(updates_ref, out_ref):
    updates = [updates_ref[r] for r in range(REPLICAS)]
    lines = []
    for i, j in PAIRS:
        product = updates[i] * updates[j]
        lines.append(jnp.sum(product, axis=0, keepdims=True))
    while len(lines) % 8:
        lines.append(jnp.zeros_like(lines[0]))
    sums = jnp.sum(jnp.concatenate(lines, axis=0), axis=1, keepdims=True)
    spread = jnp.broadcast_to(sums, (len(lines), LANES))
    line = lax.broadcasted_iota(jnp.int32, spread.shape, 0)
    lane = lax.broadcasted_iota(jnp.int32, spread.shape, 1)
    packed = jnp.sum(jnp.where(line == lane, spread, 0.0), axis=0, keepdims=True)
    for j in range(REPLICAS):
        out_ref[j] = packed


def gram_sum_kernel(parts_ref, out_ref):
    packed = jnp.sum(parts_ref[...], axis=0)
    for j in range(SIDE * SIDE):
        out_ref[j] = packed


def merge_kernel(parts_ref, updates_ref, out_ref):
    packed = jnp.sum(parts_ref[...], axis=0)
    lane = lax.broadcasted_iota(jnp.int32, packed.shape, 1)
    gram = {}
    for place, (i, j) in enumerate(PAIRS):
        value = jnp.sum(jnp.where(lane == place, packed, 0.0), axis=1, keepdims=True)
        gram[i, j] = value
        gram[j, i] = value
    members = [[r] for r in range(REPLICAS)]
    while len(members) > 1:
        merged = []
        for lower, upper in zip(members[0::2], members[1::2]):
            cross_dot = sum(gram[i, j] for i in lower for j in upper)
            lower_norm = sum(gram[i, j] for i in lower for j in lower)
            upper_norm = sum(gram[i, j] for i in upper for j in upper)
            lower_coef = 1.0 - cross_dot / (2.0 * (lower_norm + norm_eps))
            upper_coef = 1.0 - cross_dot / (2.0 * (upper_norm + norm_eps))
            scale = {**{i: lower_coef for i in lower}, **{i: upper_coef for i in upper}}
            merged.append((lower + upper, scale))
        factor = {i: scale[i] for _, scale in merged for i in scale}
        gram = {(i, j): factor[i] * factor[j] * value for (i, j), value in gram.items()}
        total = factor if len(merged) * 2 == REPLICAS else {i: total[i] * factor[i] for i in total}
        members = [group for group, _ in merged]
    result = total[0] * updates_ref[0]
    for r in range(1, REPLICAS):
        result = result + total[r] * updates_ref[r]
    out_ref[...] = result


def on_device(
    weight,
    first_moment,
    second_moment,
    token_ids,
    shared_inputs,
    private_inputs,
    shared_targets,
    private_targets,
):
    core = lax.axis_index("core")
    z = lax.axis_index("z")
    y = lax.axis_index("y")
    sum_place = jnp.where(core == 0, z, y)
    gather_place = jnp.where(core == 0, y, z)

    own = widened(shared_inputs, private_inputs[0])
    places = jnp.stack([sum_place, gather_place]).astype(jnp.int32)
    ids = token_ids[0].astype(F32).T
    targets = own_targets(places, ids, shared_targets, private_targets[0])

    pairs = []
    upward = downward = held = own
    for hop in range(3):
        if hop >= 2:
            upward, pairs[hop - 2] = lax.optimization_barrier((upward, pairs[hop - 2]))
        upward = lax.ppermute(upward, CZY, UP)
        downward = lax.ppermute(downward, CZY, DOWN)
        pairs.append(chosen_rows(ids, held, upward))
        held = downward
    upward, pairs[1] = lax.optimization_barrier((upward, pairs[1]))
    opposite = lax.ppermute(upward, CZY, UP)

    start = kernel_call(
        states_kernel, shaped(SIDE, 3 * COLS, LANES), weight, first_moment[0], second_moment[0]
    )
    start = exchange(start, CZY, GATHER_GROUPS)
    start, part = kernel_call(
        early_kernel,
        [shaped(SIDE, 3 * COLS, LANES), shaped(COLS, TOKENS)],
        places,
        start,
        targets,
        *[pair[0] for pair in pairs],
    )
    *late, parts = kernel_call(
        late_kernel,
        [shaped(TOKENS, WIDE, dtype=BF16)] * STEPS + [shaped(SIDE, COLS, LANES)],
        ids,
        start,
        held,
        opposite,
        part,
    )
    pairs.append(late)
    states = start
    for step in range(STEPS):
        parts = exchange(parts, CZY, SUM_GROUPS)
        error = kernel_call(
            functools.partial(error_kernel, step), shaped(SIDE, COLS, LANES), parts, targets
        )
        error = exchange(error, CZY, SUM_GROUPS)
        last = step == STEPS - 1
        body = functools.partial(step_kernel, step == 0, last)
        operands = (places, error, start, states, *[pair[step] for pair in pairs])
        if last:
            updates = kernel_call(body, shaped(SIDE, COLS, LANES), *operands)
        else:
            states, parts = kernel_call(
                body,
                [shaped(SIDE, 3 * COLS, LANES), shaped(SIDE, COLS, LANES)],
                *operands,
                *[pair[step + 1] for pair in pairs],
            )

    updates = exchange(updates, CZY, GATHER_GROUPS)
    turned = kernel_call(turn_kernel, shaped(REPLICAS, LANES // REPLICAS, SIDE * COLS), updates)
    updates = exchange(turned, ("x", "core"))
    gram = kernel_call(gram_kernel, shaped(REPLICAS, 1, LANES), updates)
    gram = exchange(gram, ("x", "core"))
    gram = kernel_call(gram_sum_kernel, shaped(SIDE * SIDE, 1, LANES), gram)
    gram = exchange(gram, ("z", "y"))
    return kernel_call(
        merge_kernel, shaped(LANES // REPLICAS, SIDE * COLS), gram, updates
    )


def solution(mesh):
    torus = Mesh(mesh.devices.reshape(4, 2, SIDE, SIDE), ("x", "core", "z", "y"))
    row = ("z", "y")
    rep = ("x", "core")
    placed = (
        P(row, None),
        P(rep, row, None),
        P(rep, row, None),
        P(rep, None, None),
        P(None, row),
        P(rep, None, row),
        P(),
        P(rep, None, None),
    )
    return jax.shard_map(
        on_device,
        mesh=torus,
        in_specs=placed,
        out_specs=P((*row, *rep), None),
        check_vma=False,
    )
```

```python
import functools

import jax
import jax.numpy as jnp
from jax import lax
from jax.experimental import pallas as pl
from jax.experimental.pallas import tpu as pltpu
from jax.sharding import Mesh
from jax.sharding import PartitionSpec as P

CZY = ("core", "z", "y")
F32 = jnp.float32
BF16 = jnp.bfloat16

learn_rate = 0.001
beta_one = 0.9
beta_two = 0.95
adam_eps = 1e-08
weight_decay = 0.1
norm_eps = 1e-06

SIDE = 8
LANES = 128
COLS = 48
POOL = 1024
TABLE = 1536
STEPS = 4
TOKENS = 1024
REPLICAS = 8
PAIRS = [(i, j) for i in range(REPLICAS) for j in range(i, REPLICAS)]
MIB = 1024 * 1024
WIDE = 2 * LANES
OFFSETS = (0, -1, 1, -2, 2, -3, 3, 4)


def position(core, z, y):
    return (core * SIDE + z) * SIDE + y


SUM_GROUPS = [[position(0, z, y) for z in range(SIDE)] for y in range(SIDE)] + [
    [position(1, z, y) for y in range(SIDE)] for z in range(SIDE)
]
GATHER_GROUPS = [[position(0, z, y) for y in range(SIDE)] for z in range(SIDE)] + [
    [position(1, z, y) for z in range(SIDE)] for y in range(SIDE)
]


UP = [(group[i], group[(i + 1) % SIDE]) for group in GATHER_GROUPS for i in range(SIDE)]
DOWN = [(group[i], group[(i - 1) % SIDE]) for group in GATHER_GROUPS for i in range(SIDE)]


def exchange(blocks, axes, groups=None):
    return lax.all_to_all(
        blocks, axes, split_axis=0, concat_axis=0, tiled=True, axis_index_groups=groups
    )


def kernel_call(body, out_shapes, *operands, room=12):
    in_specs = [
        pl.BlockSpec(memory_space=pltpu.SMEM if operand.dtype == jnp.int32 else pltpu.VMEM)
        for operand in operands
    ]
    return pl.pallas_call(
        body,
        in_specs=in_specs,
        out_shape=out_shapes,
        compiler_params=pltpu.CompilerParams(vmem_limit_bytes=room * MIB),
    )(*operands)


def shaped(*dims, dtype=F32):
    return jax.ShapeDtypeStruct(dims, dtype)


def product_of(left, right):
    return jnp.dot(left, right, preferred_element_type=F32)


def turned_product(left, right):
    return lax.dot_general(left, right, (((1,), (1,)), ((), ())), preferred_element_type=F32)


def store_output(out_ref, token, output):
    for half in range(2):
        out_ref[token // LANES + half] = output[:, half * LANES : (half + 1) * LANES]


def states_kernel(w_ref, m_ref, v_ref, out_ref):
    for part, ref in enumerate((w_ref, m_ref, v_ref)):
        turned = ref[...].astype(F32).T.reshape(SIDE, COLS, LANES)
        out_ref[:, part * COLS : (part + 1) * COLS, :] = turned


def widen_kernel(shared_ref, private_ref, out_ref, shared, private, arrived):
    copies = [
        pltpu.make_async_copy(shared_ref, shared, arrived.at[0]),
        pltpu.make_async_copy(private_ref, private, arrived.at[1]),
    ]
    for copy in copies:
        copy.start()
    copies[0].wait()
    out_ref[:POOL, :] = shared[...].astype(F32)
    copies[1].wait()
    out_ref[POOL:, :] = private[...].astype(F32)


def widened(shared_inputs, private_inputs):
    return pl.pallas_call(
        widen_kernel,
        in_specs=[pl.BlockSpec(memory_space=pltpu.HBM)] * 2,
        out_shape=shaped(TABLE, LANES),
        scratch_shapes=[
            pltpu.VMEM((POOL, LANES), BF16),
            pltpu.VMEM((TABLE - POOL, LANES), BF16),
            pltpu.SemaphoreType.DMA((2,)),
        ],
        compiler_params=pltpu.CompilerParams(vmem_limit_bytes=4 * MIB),
    )(shared_inputs, private_inputs)


def choice(ids, width=TABLE, start=0):
    row = lax.broadcasted_iota(jnp.int32, (ids.shape[0], width), 1).astype(F32) + start
    return jnp.where(row == ids, 1.0, 0.0).astype(BF16)


def choose(ids_ref, step, pair, out_ref):
    for token in range(0, TOKENS, WIDE):
        tokens = slice(token, token + WIDE)
        chosen = choice(ids_ref[tokens, step : step + 1])
        out_ref[tokens, :] = product_of(chosen, pair).astype(BF16)


def target_kernel(place_ref, ids_ref, shared_ref, private_ref, target_ref, turned):
    own = pl.ds(pl.multiple_of(place_ref[0] * LANES, LANES), LANES)
    columns = pl.ds(pl.multiple_of(place_ref[1] * COLS, 16), COLS)
    for step in range(STEPS):
        ids = ids_ref[own, step : step + 1]
        targets = product_of(choice(ids, POOL), shared_ref[...])
        targets = targets + product_of(choice(ids, TABLE - POOL, POOL), private_ref[...])
        turned[...] = targets.T
        target_ref[step] = turned[columns, :]


def own_targets(places, ids, shared_targets, private_targets):
    return pl.pallas_call(
        target_kernel,
        in_specs=[pl.BlockSpec(memory_space=pltpu.SMEM)]
        + [pl.BlockSpec(memory_space=pltpu.VMEM)] * 3,
        out_shape=shaped(STEPS, COLS, LANES),
        scratch_shapes=[pltpu.VMEM((SIDE * COLS, LANES), F32)],
        compiler_params=pltpu.CompilerParams(vmem_limit_bytes=12 * MIB),
    )(places, ids, shared_targets, private_targets)


def pair_of(first_ref, second_ref):
    return jnp.concatenate([first_ref[...], second_ref[...]], axis=1).astype(BF16)


def rows_kernel(ids_ref, first_ref, second_ref, now_ref, *refs):
    later, (held, left) = refs[: STEPS - 1], refs[STEPS - 1 :]
    pair = pair_of(first_ref, second_ref)
    copies = []
    for step in range(1, STEPS):
        choose(ids_ref, step, pair, held.at[step - 1])
        copies.append(pltpu.make_async_copy(held.at[step - 1], later[step - 1], left.at[step - 1]))
        copies[-1].start()
    choose(ids_ref, 0, pair, now_ref)
    for copy in copies:
        copy.wait()


def chosen_rows(ids, first, second):
    return pl.pallas_call(
        rows_kernel,
        in_specs=[pl.BlockSpec(memory_space=pltpu.VMEM)] * 3,
        out_shape=[shaped(TOKENS, WIDE, dtype=BF16)] * STEPS,
        out_specs=[pl.BlockSpec(memory_space=pltpu.VMEM)]
        + [pl.BlockSpec(memory_space=pltpu.HBM)] * (STEPS - 1),
        scratch_shapes=[
            pltpu.VMEM((STEPS - 1, TOKENS, WIDE), BF16),
            pltpu.SemaphoreType.DMA((STEPS - 1,)),
        ],
        cost_estimate=pl.CostEstimate(
            flops=2 * STEPS * TOKENS * TABLE * WIDE, bytes_accessed=4 * MIB, transcendentals=0
        ),
        compiler_params=pltpu.CompilerParams(vmem_limit_bytes=54 * MIB),
    )(ids, first, second)


def early_kernel(place_ref, start_ref, target_ref, *refs):
    pairs, (states_ref, part_ref) = refs[:3], refs[3:]
    place = place_ref[1]
    for k, offset in enumerate(OFFSETS):
        states_ref[k] = start_ref[lax.rem(place + (offset + SIDE), SIDE)]
    weights = jnp.concatenate([states_ref[k, :COLS, :] for k in range(6)], axis=1).astype(BF16)
    for token in range(0, TOKENS, WIDE):
        tokens = slice(token, token + WIDE)
        rows = jnp.concatenate([pair[tokens, :] for pair in pairs], axis=1)
        part_ref[:, tokens] = turned_product(weights, rows)


def late_kernel(ids_ref, states_ref, first_ref, second_ref, part_ref, *outs):
    out_ref = outs[STEPS]
    pair = pair_of(first_ref, second_ref)
    weights = jnp.concatenate([states_ref[k, :COLS, :] for k in (6, 7)], axis=1).astype(BF16)
    for step in range(STEPS):
        choose(ids_ref, step, pair, outs[step])
    for token in range(0, TOKENS, WIDE):
        tokens = slice(token, token + WIDE)
        output = part_ref[:, tokens] + turned_product(weights, outs[0][tokens, :])
        store_output(out_ref, token, output)


def error_kernel(step, parts_ref, target_ref, out_ref):
    output = parts_ref[0]
    for j in range(1, SIDE):
        output = output + parts_ref[j]
    error = (output - target_ref[step]).astype(BF16).astype(F32)
    for j in range(SIDE):
        out_ref[j] = error


def step_kernel(first, last, place_ref, error_ref, w_ref, states_ref, *refs):
    pairs, rest = refs[: SIDE // 2], refs[SIDE // 2 :]
    if last:
        (total_out,) = rest
        place = place_ref[1]
    else:
        next_pairs, (new_states, output_ref) = rest[: SIDE // 2], rest[SIDE // 2 :]
    error = jnp.concatenate([error_ref[j] for j in range(SIDE)], axis=1).astype(BF16)
    updated = []
    for k in range(SIDE // 2):
        gradients = product_of(error, pairs[k][...]) * (1.0 / TOKENS)
        for half in range(2):
            j = 2 * k + half
            gradient = gradients[:, half * LANES : (half + 1) * LANES]
            weight_start = w_ref[j, :COLS, :]
            if first:
                weight_now = weight_start
            else:
                update_sum = states_ref[j, 2 * COLS :, :]
                weight_now = weight_start - learn_rate * update_sum
            base = COLS if first else 0
            moment_one = states_ref[j, base : base + COLS, :]
            moment_two = states_ref[j, base + COLS : base + 2 * COLS, :]
            moment_one = beta_one * moment_one + (1.0 - beta_one) * gradient
            moment_two = beta_two * moment_two + (1.0 - beta_two) * gradient * gradient
            direction = (
                moment_one / (jnp.sqrt(moment_two) + adam_eps) + weight_decay * weight_now
            )
            update_sum = direction if first else update_sum + direction
            if last:
                total_out[lax.rem(place + (OFFSETS[j] + SIDE), SIDE)] = update_sum
            else:
                new_states[j, :COLS, :] = moment_one
                new_states[j, COLS : 2 * COLS, :] = moment_two
                new_states[j, 2 * COLS :, :] = update_sum
                updated.append((weight_start - learn_rate * update_sum).astype(BF16))
    if last:
        return
    weights = jnp.concatenate(updated, axis=1)
    for token in range(0, TOKENS, WIDE):
        tokens = slice(token, token + WIDE)
        rows = jnp.concatenate([pair[tokens, :] for pair in next_pairs], axis=1)
        store_output(output_ref, token, turned_product(weights, rows))


def turn_kernel(parts_ref, out_ref):
    turned = parts_ref[...].reshape(SIDE * COLS, LANES).T
    out_ref[...] = turned.reshape(REPLICAS, LANES // REPLICAS, SIDE * COLS)


def gram_kernel(updates_ref, out_ref):
    updates = [updates_ref[r] for r in range(REPLICAS)]
    lines = []
    for i, j in PAIRS:
        product = updates[i] * updates[j]
        lines.append(jnp.sum(product, axis=0, keepdims=True))
    while len(lines) % 8:
        lines.append(jnp.zeros_like(lines[0]))
    sums = jnp.sum(jnp.concatenate(lines, axis=0), axis=1, keepdims=True)
    spread = jnp.broadcast_to(sums, (len(lines), LANES))
    line = lax.broadcasted_iota(jnp.int32, spread.shape, 0)
    lane = lax.broadcasted_iota(jnp.int32, spread.shape, 1)
    packed = jnp.sum(jnp.where(line == lane, spread, 0.0), axis=0, keepdims=True)
    for j in range(REPLICAS):
        out_ref[j] = packed


def gram_sum_kernel(parts_ref, out_ref):
    packed = jnp.sum(parts_ref[...], axis=0)
    for j in range(SIDE * SIDE):
        out_ref[j] = packed


def merge_kernel(parts_ref, updates_ref, out_ref):
    packed = jnp.sum(parts_ref[...], axis=0)
    lane = lax.broadcasted_iota(jnp.int32, packed.shape, 1)
    gram = {}
    for place, (i, j) in enumerate(PAIRS):
        value = jnp.sum(jnp.where(lane == place, packed, 0.0), axis=1, keepdims=True)
        gram[i, j] = value
        gram[j, i] = value
    members = [[r] for r in range(REPLICAS)]
    while len(members) > 1:
        merged = []
        for lower, upper in zip(members[0::2], members[1::2]):
            cross_dot = sum(gram[i, j] for i in lower for j in upper)
            lower_norm = sum(gram[i, j] for i in lower for j in lower)
            upper_norm = sum(gram[i, j] for i in upper for j in upper)
            lower_coef = 1.0 - cross_dot / (2.0 * (lower_norm + norm_eps))
            upper_coef = 1.0 - cross_dot / (2.0 * (upper_norm + norm_eps))
            scale = {**{i: lower_coef for i in lower}, **{i: upper_coef for i in upper}}
            merged.append((lower + upper, scale))
        factor = {i: scale[i] for _, scale in merged for i in scale}
        gram = {(i, j): factor[i] * factor[j] * value for (i, j), value in gram.items()}
        total = factor if len(merged) * 2 == REPLICAS else {i: total[i] * factor[i] for i in total}
        members = [group for group, _ in merged]
    result = total[0] * updates_ref[0]
    for r in range(1, REPLICAS):
        result = result + total[r] * updates_ref[r]
    out_ref[...] = result


def on_device(
    weight,
    first_moment,
    second_moment,
    token_ids,
    shared_inputs,
    private_inputs,
    shared_targets,
    private_targets,
):
    core = lax.axis_index("core")
    z = lax.axis_index("z")
    y = lax.axis_index("y")
    sum_place = jnp.where(core == 0, z, y)
    gather_place = jnp.where(core == 0, y, z)

    own = widened(shared_inputs, private_inputs[0])
    places = jnp.stack([sum_place, gather_place]).astype(jnp.int32)
    ids = token_ids[0].astype(F32).T
    targets = own_targets(places, ids, shared_targets, private_targets[0])

    pairs = []
    upward = downward = held = own
    for hop in range(3):
        if hop >= 2:
            upward, pairs[hop - 2] = lax.optimization_barrier((upward, pairs[hop - 2]))
        upward = lax.ppermute(upward, CZY, UP)
        downward = lax.ppermute(downward, CZY, DOWN)
        pairs.append(chosen_rows(ids, held, upward))
        held = downward
    upward, pairs[1] = lax.optimization_barrier((upward, pairs[1]))
    opposite = lax.ppermute(upward, CZY, UP)

    start = kernel_call(
        states_kernel, shaped(SIDE, 3 * COLS, LANES), weight, first_moment[0], second_moment[0]
    )
    start = exchange(start, CZY, GATHER_GROUPS)
    start, part = kernel_call(
        early_kernel,
        [shaped(SIDE, 3 * COLS, LANES), shaped(COLS, TOKENS)],
        places,
        start,
        targets,
        *[pair[0] for pair in pairs],
    )
    *late, parts = kernel_call(
        late_kernel,
        [shaped(TOKENS, WIDE, dtype=BF16)] * STEPS + [shaped(SIDE, COLS, LANES)],
        ids,
        start,
        held,
        opposite,
        part,
    )
    pairs.append(late)
    states = start
    for step in range(STEPS):
        parts = exchange(parts, CZY, SUM_GROUPS)
        error = kernel_call(
            functools.partial(error_kernel, step), shaped(SIDE, COLS, LANES), parts, targets
        )
        error = exchange(error, CZY, SUM_GROUPS)
        last = step == STEPS - 1
        body = functools.partial(step_kernel, step == 0, last)
        operands = (places, error, start, states, *[pair[step] for pair in pairs])
        if last:
            updates = kernel_call(body, shaped(SIDE, COLS, LANES), *operands)
        else:
            states, parts = kernel_call(
                body,
                [shaped(SIDE, 3 * COLS, LANES), shaped(SIDE, COLS, LANES)],
                *operands,
                *[pair[step + 1] for pair in pairs],
            )

    updates = exchange(updates, CZY, GATHER_GROUPS)
    turned = kernel_call(turn_kernel, shaped(REPLICAS, LANES // REPLICAS, SIDE * COLS), updates)
    updates = exchange(turned, ("x", "core"))
    gram = kernel_call(gram_kernel, shaped(REPLICAS, 1, LANES), updates)
    gram = exchange(gram, ("x", "core"))
    gram = kernel_call(gram_sum_kernel, shaped(SIDE * SIDE, 1, LANES), gram)
    gram = exchange(gram, ("z", "y"))
    return kernel_call(
        merge_kernel, shaped(LANES // REPLICAS, SIDE * COLS), gram, updates
    )


def solution(mesh):
    torus = Mesh(mesh.devices.reshape(4, 2, SIDE, SIDE), ("x", "core", "z", "y"))
    row = ("z", "y")
    rep = ("x", "core")
    placed = (
        P(row, None),
        P(rep, row, None),
        P(rep, row, None),
        P(rep, None, None),
        P(None, row),
        P(rep, None, row),
        P(),
        P(rep, None, None),
    )
    return jax.shard_map(
        on_device,
        mesh=torus,
        in_specs=placed,
        out_specs=P((*row, *rep), None),
        check_vma=False,
    )
```

```python
import functools

import jax
import jax.numpy as jnp
from jax import lax
from jax.experimental import pallas as pl
from jax.experimental.pallas import tpu as pltpu
from jax.sharding import Mesh
from jax.sharding import PartitionSpec as P

CZY = ("core", "z", "y")
F32 = jnp.float32
BF16 = jnp.bfloat16

learn_rate = 0.001
beta_one = 0.9
beta_two = 0.95
adam_eps = 1e-08
weight_decay = 0.1
norm_eps = 1e-06

SIDE = 8
LANES = 128
COLS = 48
POOL = 1024
TABLE = 1536
STEPS = 4
TOKENS = 1024
REPLICAS = 8
PAIRS = [(i, j) for i in range(REPLICAS) for j in range(i, REPLICAS)]
MIB = 1024 * 1024
WIDE = 2 * LANES
OFFSETS = (0, -1, 1, -2, 2, -3, 3, 4)


def position(core, z, y):
    return (core * SIDE + z) * SIDE + y


SUM_GROUPS = [[position(0, z, y) for z in range(SIDE)] for y in range(SIDE)] + [
    [position(1, z, y) for y in range(SIDE)] for z in range(SIDE)
]
GATHER_GROUPS = [[position(0, z, y) for y in range(SIDE)] for z in range(SIDE)] + [
    [position(1, z, y) for z in range(SIDE)] for y in range(SIDE)
]


UP = [(group[i], group[(i + 1) % SIDE]) for group in GATHER_GROUPS for i in range(SIDE)]
DOWN = [(group[i], group[(i - 1) % SIDE]) for group in GATHER_GROUPS for i in range(SIDE)]


def exchange(blocks, axes, groups=None):
    return lax.all_to_all(
        blocks, axes, split_axis=0, concat_axis=0, tiled=True, axis_index_groups=groups
    )


def kernel_call(body, out_shapes, *operands, room=12):
    in_specs = [
        pl.BlockSpec(memory_space=pltpu.SMEM if operand.dtype == jnp.int32 else pltpu.VMEM)
        for operand in operands
    ]
    return pl.pallas_call(
        body,
        in_specs=in_specs,
        out_shape=out_shapes,
        compiler_params=pltpu.CompilerParams(vmem_limit_bytes=room * MIB),
    )(*operands)


def shaped(*dims, dtype=F32):
    return jax.ShapeDtypeStruct(dims, dtype)


def product_of(left, right):
    return jnp.dot(left, right, preferred_element_type=F32)


def turned_product(left, right):
    return lax.dot_general(left, right, (((1,), (1,)), ((), ())), preferred_element_type=F32)


def store_output(out_ref, token, output):
    for half in range(2):
        out_ref[token // LANES + half] = output[:, half * LANES : (half + 1) * LANES]


def states_kernel(w_ref, m_ref, v_ref, out_ref):
    for part, ref in enumerate((w_ref, m_ref, v_ref)):
        turned = ref[...].astype(F32).T.reshape(SIDE, COLS, LANES)
        out_ref[:, part * COLS : (part + 1) * COLS, :] = turned


def widen_kernel(shared_ref, private_ref, out_ref, shared, private, arrived):
    copies = [
        pltpu.make_async_copy(shared_ref, shared, arrived.at[0]),
        pltpu.make_async_copy(private_ref, private, arrived.at[1]),
    ]
    for copy in copies:
        copy.start()
    copies[0].wait()
    out_ref[:POOL, :] = shared[...].astype(F32)
    copies[1].wait()
    out_ref[POOL:, :] = private[...].astype(F32)


def widened(shared_inputs, private_inputs):
    return pl.pallas_call(
        widen_kernel,
        in_specs=[pl.BlockSpec(memory_space=pltpu.HBM)] * 2,
        out_shape=shaped(TABLE, LANES),
        scratch_shapes=[
            pltpu.VMEM((POOL, LANES), BF16),
            pltpu.VMEM((TABLE - POOL, LANES), BF16),
            pltpu.SemaphoreType.DMA((2,)),
        ],
        compiler_params=pltpu.CompilerParams(vmem_limit_bytes=4 * MIB),
    )(shared_inputs, private_inputs)


def choice(ids, width=TABLE, start=0):
    row = lax.broadcasted_iota(jnp.int32, (ids.shape[0], width), 1).astype(F32) + start
    return jnp.where(row == ids, 1.0, 0.0).astype(BF16)


def choose(ids_ref, step, pair, out_ref):
    for token in range(0, TOKENS, WIDE):
        tokens = slice(token, token + WIDE)
        chosen = choice(ids_ref[tokens, step : step + 1])
        out_ref[tokens, :] = product_of(chosen, pair).astype(BF16)


def target_kernel(place_ref, ids_ref, shared_ref, private_ref, target_ref, turned):
    own = pl.ds(pl.multiple_of(place_ref[0] * LANES, LANES), LANES)
    columns = pl.ds(pl.multiple_of(place_ref[1] * COLS, 16), COLS)
    for step in range(STEPS):
        ids = ids_ref[own, step : step + 1]
        targets = product_of(choice(ids, POOL), shared_ref[...])
        targets = targets + product_of(choice(ids, TABLE - POOL, POOL), private_ref[...])
        turned[...] = targets.T
        target_ref[step] = turned[columns, :]


def own_targets(places, ids, shared_targets, private_targets):
    return pl.pallas_call(
        target_kernel,
        in_specs=[pl.BlockSpec(memory_space=pltpu.SMEM)]
        + [pl.BlockSpec(memory_space=pltpu.VMEM)] * 3,
        out_shape=shaped(STEPS, COLS, LANES),
        scratch_shapes=[pltpu.VMEM((SIDE * COLS, LANES), F32)],
        compiler_params=pltpu.CompilerParams(vmem_limit_bytes=12 * MIB),
    )(places, ids, shared_targets, private_targets)


def pair_of(first_ref, second_ref):
    return jnp.concatenate([first_ref[...], second_ref[...]], axis=1).astype(BF16)


def rows_kernel(ids_ref, first_ref, second_ref, now_ref, *refs):
    later, (held, left) = refs[: STEPS - 1], refs[STEPS - 1 :]
    pair = pair_of(first_ref, second_ref)
    copies = []
    for step in range(1, STEPS):
        choose(ids_ref, step, pair, held.at[step - 1])
        copies.append(pltpu.make_async_copy(held.at[step - 1], later[step - 1], left.at[step - 1]))
        copies[-1].start()
    choose(ids_ref, 0, pair, now_ref)
    for copy in copies:
        copy.wait()


def chosen_rows(ids, first, second):
    return pl.pallas_call(
        rows_kernel,
        in_specs=[pl.BlockSpec(memory_space=pltpu.VMEM)] * 3,
        out_shape=[shaped(TOKENS, WIDE, dtype=BF16)] * STEPS,
        out_specs=[pl.BlockSpec(memory_space=pltpu.VMEM)]
        + [pl.BlockSpec(memory_space=pltpu.HBM)] * (STEPS - 1),
        scratch_shapes=[
            pltpu.VMEM((STEPS - 1, TOKENS, WIDE), BF16),
            pltpu.SemaphoreType.DMA((STEPS - 1,)),
        ],
        cost_estimate=pl.CostEstimate(
            flops=2 * STEPS * TOKENS * TABLE * WIDE, bytes_accessed=4 * MIB, transcendentals=0
        ),
        compiler_params=pltpu.CompilerParams(vmem_limit_bytes=54 * MIB),
    )(ids, first, second)


def early_kernel(place_ref, start_ref, target_ref, *refs):
    pairs, (states_ref, part_ref) = refs[:3], refs[3:]
    place = place_ref[1]
    for k, offset in enumerate(OFFSETS):
        states_ref[k] = start_ref[lax.rem(place + (offset + SIDE), SIDE)]
    weights = jnp.concatenate([states_ref[k, :COLS, :] for k in range(6)], axis=1).astype(BF16)
    for token in range(0, TOKENS, WIDE):
        tokens = slice(token, token + WIDE)
        rows = jnp.concatenate([pair[tokens, :] for pair in pairs], axis=1)
        part_ref[:, tokens] = turned_product(weights, rows)


def late_kernel(ids_ref, states_ref, first_ref, second_ref, part_ref, now_ref, out_ref):
    choose(ids_ref, 0, pair_of(first_ref, second_ref), now_ref)
    weights = jnp.concatenate([states_ref[k, :COLS, :] for k in (6, 7)], axis=1).astype(BF16)
    for token in range(0, TOKENS, WIDE):
        tokens = slice(token, token + WIDE)
        output = part_ref[:, tokens] + turned_product(weights, now_ref[tokens, :])
        store_output(out_ref, token, output)


def rest_kernel(ids_ref, first_ref, second_ref, *later):
    pair = pair_of(first_ref, second_ref)
    for step in range(1, STEPS):
        choose(ids_ref, step, pair, later[step - 1])


def rest_rows(ids, first, second):
    return pl.pallas_call(
        rest_kernel,
        in_specs=[pl.BlockSpec(memory_space=pltpu.VMEM)] * 3,
        out_shape=[shaped(TOKENS, WIDE, dtype=BF16)] * (STEPS - 1),
        cost_estimate=pl.CostEstimate(
            flops=2 * STEPS * TOKENS * TABLE * WIDE, bytes_accessed=4 * MIB, transcendentals=0
        ),
        compiler_params=pltpu.CompilerParams(vmem_limit_bytes=12 * MIB),
    )(ids, first, second)


def error_kernel(step, parts_ref, target_ref, out_ref):
    output = parts_ref[0]
    for j in range(1, SIDE):
        output = output + parts_ref[j]
    error = (output - target_ref[step]).astype(BF16).astype(F32)
    for j in range(SIDE):
        out_ref[j] = error


def step_kernel(first, last, place_ref, error_ref, w_ref, states_ref, *refs):
    pairs, rest = refs[: SIDE // 2], refs[SIDE // 2 :]
    if last:
        (total_out,) = rest
        place = place_ref[1]
    else:
        next_pairs, (new_states, output_ref) = rest[: SIDE // 2], rest[SIDE // 2 :]
    error = jnp.concatenate([error_ref[j] for j in range(SIDE)], axis=1).astype(BF16)
    updated = []
    for k in range(SIDE // 2):
        gradients = product_of(error, pairs[k][...]) * (1.0 / TOKENS)
        for half in range(2):
            j = 2 * k + half
            gradient = gradients[:, half * LANES : (half + 1) * LANES]
            weight_start = w_ref[j, :COLS, :]
            if first:
                weight_now = weight_start
            else:
                update_sum = states_ref[j, 2 * COLS :, :]
                weight_now = weight_start - learn_rate * update_sum
            base = COLS if first else 0
            moment_one = states_ref[j, base : base + COLS, :]
            moment_two = states_ref[j, base + COLS : base + 2 * COLS, :]
            moment_one = beta_one * moment_one + (1.0 - beta_one) * gradient
            moment_two = beta_two * moment_two + (1.0 - beta_two) * gradient * gradient
            direction = (
                moment_one / (jnp.sqrt(moment_two) + adam_eps) + weight_decay * weight_now
            )
            update_sum = direction if first else update_sum + direction
            if last:
                total_out[lax.rem(place + (OFFSETS[j] + SIDE), SIDE)] = update_sum
            else:
                new_states[j, :COLS, :] = moment_one
                new_states[j, COLS : 2 * COLS, :] = moment_two
                new_states[j, 2 * COLS :, :] = update_sum
                updated.append((weight_start - learn_rate * update_sum).astype(BF16))
    if last:
        return
    weights = jnp.concatenate(updated, axis=1)
    for token in range(0, TOKENS, WIDE):
        tokens = slice(token, token + WIDE)
        rows = jnp.concatenate([pair[tokens, :] for pair in next_pairs], axis=1)
        store_output(output_ref, token, turned_product(weights, rows))


def turn_kernel(parts_ref, out_ref):
    turned = parts_ref[...].reshape(SIDE * COLS, LANES).T
    out_ref[...] = turned.reshape(REPLICAS, LANES // REPLICAS, SIDE * COLS)


def gram_kernel(updates_ref, out_ref):
    updates = [updates_ref[r] for r in range(REPLICAS)]
    lines = []
    for i, j in PAIRS:
        product = updates[i] * updates[j]
        lines.append(jnp.sum(product, axis=0, keepdims=True))
    while len(lines) % 8:
        lines.append(jnp.zeros_like(lines[0]))
    sums = jnp.sum(jnp.concatenate(lines, axis=0), axis=1, keepdims=True)
    spread = jnp.broadcast_to(sums, (len(lines), LANES))
    line = lax.broadcasted_iota(jnp.int32, spread.shape, 0)
    lane = lax.broadcasted_iota(jnp.int32, spread.shape, 1)
    packed = jnp.sum(jnp.where(line == lane, spread, 0.0), axis=0, keepdims=True)
    for j in range(REPLICAS):
        out_ref[j] = packed


def gram_sum_kernel(parts_ref, out_ref):
    packed = jnp.sum(parts_ref[...], axis=0)
    for j in range(SIDE * SIDE):
        out_ref[j] = packed


def merge_kernel(parts_ref, updates_ref, out_ref):
    packed = jnp.sum(parts_ref[...], axis=0)
    lane = lax.broadcasted_iota(jnp.int32, packed.shape, 1)
    gram = {}
    for place, (i, j) in enumerate(PAIRS):
        value = jnp.sum(jnp.where(lane == place, packed, 0.0), axis=1, keepdims=True)
        gram[i, j] = value
        gram[j, i] = value
    members = [[r] for r in range(REPLICAS)]
    while len(members) > 1:
        merged = []
        for lower, upper in zip(members[0::2], members[1::2]):
            cross_dot = sum(gram[i, j] for i in lower for j in upper)
            lower_norm = sum(gram[i, j] for i in lower for j in lower)
            upper_norm = sum(gram[i, j] for i in upper for j in upper)
            lower_coef = 1.0 - cross_dot / (2.0 * (lower_norm + norm_eps))
            upper_coef = 1.0 - cross_dot / (2.0 * (upper_norm + norm_eps))
            scale = {**{i: lower_coef for i in lower}, **{i: upper_coef for i in upper}}
            merged.append((lower + upper, scale))
        factor = {i: scale[i] for _, scale in merged for i in scale}
        gram = {(i, j): factor[i] * factor[j] * value for (i, j), value in gram.items()}
        total = factor if len(merged) * 2 == REPLICAS else {i: total[i] * factor[i] for i in total}
        members = [group for group, _ in merged]
    result = total[0] * updates_ref[0]
    for r in range(1, REPLICAS):
        result = result + total[r] * updates_ref[r]
    out_ref[...] = result


def on_device(
    weight,
    first_moment,
    second_moment,
    token_ids,
    shared_inputs,
    private_inputs,
    shared_targets,
    private_targets,
):
    core = lax.axis_index("core")
    z = lax.axis_index("z")
    y = lax.axis_index("y")
    sum_place = jnp.where(core == 0, z, y)
    gather_place = jnp.where(core == 0, y, z)

    own = widened(shared_inputs, private_inputs[0])
    places = jnp.stack([sum_place, gather_place]).astype(jnp.int32)
    ids = token_ids[0].astype(F32).T
    targets = own_targets(places, ids, shared_targets, private_targets[0])

    pairs = []
    upward = downward = held = own
    for hop in range(3):
        if hop >= 2:
            upward, pairs[hop - 2] = lax.optimization_barrier((upward, pairs[hop - 2]))
        upward = lax.ppermute(upward, CZY, UP)
        downward = lax.ppermute(downward, CZY, DOWN)
        pairs.append(chosen_rows(ids, held, upward))
        held = downward
    upward, pairs[1] = lax.optimization_barrier((upward, pairs[1]))
    opposite = lax.ppermute(upward, CZY, UP)

    start = kernel_call(
        states_kernel, shaped(SIDE, 3 * COLS, LANES), weight, first_moment[0], second_moment[0]
    )
    start = exchange(start, CZY, GATHER_GROUPS)
    start, part = kernel_call(
        early_kernel,
        [shaped(SIDE, 3 * COLS, LANES), shaped(COLS, TOKENS)],
        places,
        start,
        targets,
        *[pair[0] for pair in pairs],
    )
    now, parts = kernel_call(
        late_kernel,
        [shaped(TOKENS, WIDE, dtype=BF16), shaped(SIDE, COLS, LANES)],
        ids,
        start,
        held,
        opposite,
        part,
    )
    pairs.append([now, *rest_rows(ids, held, opposite)])
    states = start
    for step in range(STEPS):
        parts = exchange(parts, CZY, SUM_GROUPS)
        error = kernel_call(
            functools.partial(error_kernel, step), shaped(SIDE, COLS, LANES), parts, targets
        )
        error = exchange(error, CZY, SUM_GROUPS)
        last = step == STEPS - 1
        body = functools.partial(step_kernel, step == 0, last)
        operands = (places, error, start, states, *[pair[step] for pair in pairs])
        if last:
            updates = kernel_call(body, shaped(SIDE, COLS, LANES), *operands)
        else:
            states, parts = kernel_call(
                body,
                [shaped(SIDE, 3 * COLS, LANES), shaped(SIDE, COLS, LANES)],
                *operands,
                *[pair[step + 1] for pair in pairs],
            )

    updates = exchange(updates, CZY, GATHER_GROUPS)
    turned = kernel_call(turn_kernel, shaped(REPLICAS, LANES // REPLICAS, SIDE * COLS), updates)
    updates = exchange(turned, ("x", "core"))
    gram = kernel_call(gram_kernel, shaped(REPLICAS, 1, LANES), updates)
    gram = exchange(gram, ("x", "core"))
    gram = kernel_call(gram_sum_kernel, shaped(SIDE * SIDE, 1, LANES), gram)
    gram = exchange(gram, ("z", "y"))
    return kernel_call(
        merge_kernel, shaped(LANES // REPLICAS, SIDE * COLS), gram, updates
    )


def solution(mesh):
    torus = Mesh(mesh.devices.reshape(4, 2, SIDE, SIDE), ("x", "core", "z", "y"))
    row = ("z", "y")
    rep = ("x", "core")
    placed = (
        P(row, None),
        P(rep, row, None),
        P(rep, row, None),
        P(rep, None, None),
        P(None, row),
        P(rep, None, row),
        P(),
        P(rep, None, None),
    )
    return jax.shard_map(
        on_device,
        mesh=torus,
        in_specs=placed,
        out_specs=P((*row, *rep), None),
        check_vma=False,
    )
```

```python
import functools

import jax
import jax.numpy as jnp
from jax import lax
from jax.experimental import pallas as pl
from jax.experimental.pallas import tpu as pltpu
from jax.sharding import Mesh
from jax.sharding import PartitionSpec as P

CZY = ("core", "z", "y")
F32 = jnp.float32
BF16 = jnp.bfloat16

learn_rate = 0.001
beta_one = 0.9
beta_two = 0.95
adam_eps = 1e-08
weight_decay = 0.1
norm_eps = 1e-06

SIDE = 8
LANES = 128
COLS = 48
POOL = 1024
TABLE = 1536
STEPS = 4
TOKENS = 1024
REPLICAS = 8
PAIRS = [(i, j) for i in range(REPLICAS) for j in range(i, REPLICAS)]
MIB = 1024 * 1024
WIDE = 2 * LANES
OFFSETS = (0, -1, 1, -2, 2, -3, 3, 4)


def position(core, z, y):
    return (core * SIDE + z) * SIDE + y


SUM_GROUPS = [[position(0, z, y) for z in range(SIDE)] for y in range(SIDE)] + [
    [position(1, z, y) for y in range(SIDE)] for z in range(SIDE)
]
GATHER_GROUPS = [[position(0, z, y) for y in range(SIDE)] for z in range(SIDE)] + [
    [position(1, z, y) for z in range(SIDE)] for y in range(SIDE)
]


UP = [(group[i], group[(i + 1) % SIDE]) for group in GATHER_GROUPS for i in range(SIDE)]
DOWN = [(group[i], group[(i - 1) % SIDE]) for group in GATHER_GROUPS for i in range(SIDE)]


def exchange(blocks, axes, groups=None):
    return lax.all_to_all(
        blocks, axes, split_axis=0, concat_axis=0, tiled=True, axis_index_groups=groups
    )


def kernel_call(body, out_shapes, *operands, room=12):
    in_specs = [
        pl.BlockSpec(memory_space=pltpu.SMEM if operand.dtype == jnp.int32 else pltpu.VMEM)
        for operand in operands
    ]
    return pl.pallas_call(
        body,
        in_specs=in_specs,
        out_shape=out_shapes,
        compiler_params=pltpu.CompilerParams(vmem_limit_bytes=room * MIB),
    )(*operands)


def shaped(*dims, dtype=F32):
    return jax.ShapeDtypeStruct(dims, dtype)


def product_of(left, right):
    return jnp.dot(left, right, preferred_element_type=F32)


def turned_product(left, right):
    return lax.dot_general(left, right, (((1,), (1,)), ((), ())), preferred_element_type=F32)


def store_output(out_ref, token, output):
    for half in range(2):
        out_ref[token // LANES + half] = output[:, half * LANES : (half + 1) * LANES]


def states_kernel(w_ref, m_ref, v_ref, out_ref):
    for part, ref in enumerate((w_ref, m_ref, v_ref)):
        turned = ref[...].astype(F32).T.reshape(SIDE, COLS, LANES)
        out_ref[:, part * COLS : (part + 1) * COLS, :] = turned


def widen_kernel(shared_ref, private_ref, out_ref, shared, private, arrived):
    copies = [
        pltpu.make_async_copy(shared_ref, shared, arrived.at[0]),
        pltpu.make_async_copy(private_ref, private, arrived.at[1]),
    ]
    for copy in copies:
        copy.start()
    copies[0].wait()
    out_ref[:POOL, :] = shared[...].astype(F32)
    copies[1].wait()
    out_ref[POOL:, :] = private[...].astype(F32)


def widened(shared_inputs, private_inputs):
    return pl.pallas_call(
        widen_kernel,
        in_specs=[pl.BlockSpec(memory_space=pltpu.HBM)] * 2,
        out_shape=shaped(TABLE, LANES),
        scratch_shapes=[
            pltpu.VMEM((POOL, LANES), BF16),
            pltpu.VMEM((TABLE - POOL, LANES), BF16),
            pltpu.SemaphoreType.DMA((2,)),
        ],
        compiler_params=pltpu.CompilerParams(vmem_limit_bytes=4 * MIB),
    )(shared_inputs, private_inputs)


def choice(ids, width=TABLE, start=0):
    row = lax.broadcasted_iota(jnp.int32, (ids.shape[0], width), 1).astype(F32) + start
    return jnp.where(row == ids, 1.0, 0.0).astype(BF16)


def choose(ids_ref, step, pair, out_ref):
    for token in range(0, TOKENS, WIDE):
        tokens = slice(token, token + WIDE)
        chosen = choice(ids_ref[tokens, step : step + 1])
        out_ref[tokens, :] = product_of(chosen, pair).astype(BF16)


def target_kernel(place_ref, ids_ref, shared_ref, private_ref, target_ref, turned):
    own = pl.ds(pl.multiple_of(place_ref[0] * LANES, LANES), LANES)
    columns = pl.ds(pl.multiple_of(place_ref[1] * COLS, 16), COLS)
    for step in range(STEPS):
        ids = ids_ref[own, step : step + 1]
        targets = product_of(choice(ids, POOL), shared_ref[...])
        targets = targets + product_of(choice(ids, TABLE - POOL, POOL), private_ref[...])
        turned[...] = targets.T
        target_ref[step] = turned[columns, :]


def own_targets(places, ids, shared_targets, private_targets):
    return pl.pallas_call(
        target_kernel,
        in_specs=[pl.BlockSpec(memory_space=pltpu.SMEM)]
        + [pl.BlockSpec(memory_space=pltpu.VMEM)] * 3,
        out_shape=shaped(STEPS, COLS, LANES),
        scratch_shapes=[pltpu.VMEM((SIDE * COLS, LANES), F32)],
        compiler_params=pltpu.CompilerParams(vmem_limit_bytes=12 * MIB),
    )(places, ids, shared_targets, private_targets)


def pair_of(first_ref, second_ref):
    return jnp.concatenate([first_ref[...], second_ref[...]], axis=1).astype(BF16)


def rows_kernel(steps, ids_ref, first_ref, second_ref, *refs):
    outs, (held, left) = refs[: len(steps)], refs[len(steps) :]
    pair = pair_of(first_ref, second_ref)
    copies = []
    for place, step in enumerate(steps):
        choose(ids_ref, step, pair, held.at[place])
        copies.append(pltpu.make_async_copy(held.at[place], outs[place], left.at[place]))
        copies[-1].start()
    for copy in copies:
        copy.wait()


def chosen_rows(ids, first, second, steps):
    return pl.pallas_call(
        functools.partial(rows_kernel, steps),
        in_specs=[pl.BlockSpec(memory_space=pltpu.VMEM)] * 3,
        out_shape=[shaped(TOKENS, WIDE, dtype=BF16)] * len(steps),
        out_specs=[pl.BlockSpec(memory_space=pltpu.HBM)] * len(steps),
        scratch_shapes=[
            pltpu.VMEM((len(steps), TOKENS, WIDE), BF16),
            pltpu.SemaphoreType.DMA((len(steps),)),
        ],
        cost_estimate=pl.CostEstimate(
            flops=2 * len(steps) * TOKENS * TABLE * WIDE,
            bytes_accessed=len(steps) * MIB,
            transcendentals=0,
        ),
        compiler_params=pltpu.CompilerParams(vmem_limit_bytes=54 * MIB),
    )(ids, first, second)


def early_kernel(place_ref, start_ref, target_ref, *refs):
    pairs, (states_ref, part_ref) = refs[:3], refs[3:]
    place = place_ref[1]
    for k, offset in enumerate(OFFSETS):
        states_ref[k] = start_ref[lax.rem(place + (offset + SIDE), SIDE)]
    weights = jnp.concatenate([states_ref[k, :COLS, :] for k in range(6)], axis=1).astype(BF16)
    for token in range(0, TOKENS, WIDE):
        tokens = slice(token, token + WIDE)
        rows = jnp.concatenate([pair[tokens, :] for pair in pairs], axis=1)
        part_ref[:, tokens] = turned_product(weights, rows)


def late_kernel(ids_ref, states_ref, first_ref, second_ref, part_ref, *outs):
    out_ref = outs[STEPS]
    pair = pair_of(first_ref, second_ref)
    weights = jnp.concatenate([states_ref[k, :COLS, :] for k in (6, 7)], axis=1).astype(BF16)
    for step in range(STEPS):
        choose(ids_ref, step, pair, outs[step])
    for token in range(0, TOKENS, WIDE):
        tokens = slice(token, token + WIDE)
        output = part_ref[:, tokens] + turned_product(weights, outs[0][tokens, :])
        store_output(out_ref, token, output)


def error_kernel(step, parts_ref, target_ref, out_ref):
    output = parts_ref[0]
    for j in range(1, SIDE):
        output = output + parts_ref[j]
    error = (output - target_ref[step]).astype(BF16).astype(F32)
    for j in range(SIDE):
        out_ref[j] = error


def step_kernel(first, last, place_ref, error_ref, w_ref, states_ref, *refs):
    pairs, rest = refs[: SIDE // 2], refs[SIDE // 2 :]
    if last:
        (total_out,) = rest
        place = place_ref[1]
    else:
        next_pairs, (new_states, output_ref) = rest[: SIDE // 2], rest[SIDE // 2 :]
    error = jnp.concatenate([error_ref[j] for j in range(SIDE)], axis=1).astype(BF16)
    updated = []
    for k in range(SIDE // 2):
        gradients = product_of(error, pairs[k][...]) * (1.0 / TOKENS)
        for half in range(2):
            j = 2 * k + half
            gradient = gradients[:, half * LANES : (half + 1) * LANES]
            weight_start = w_ref[j, :COLS, :]
            if first:
                weight_now = weight_start
            else:
                update_sum = states_ref[j, 2 * COLS :, :]
                weight_now = weight_start - learn_rate * update_sum
            base = COLS if first else 0
            moment_one = states_ref[j, base : base + COLS, :]
            moment_two = states_ref[j, base + COLS : base + 2 * COLS, :]
            moment_one = beta_one * moment_one + (1.0 - beta_one) * gradient
            moment_two = beta_two * moment_two + (1.0 - beta_two) * gradient * gradient
            direction = (
                moment_one / (jnp.sqrt(moment_two) + adam_eps) + weight_decay * weight_now
            )
            update_sum = direction if first else update_sum + direction
            if last:
                total_out[lax.rem(place + (OFFSETS[j] + SIDE), SIDE)] = update_sum
            else:
                new_states[j, :COLS, :] = moment_one
                new_states[j, COLS : 2 * COLS, :] = moment_two
                new_states[j, 2 * COLS :, :] = update_sum
                updated.append((weight_start - learn_rate * update_sum).astype(BF16))
    if last:
        return
    weights = jnp.concatenate(updated, axis=1)
    for token in range(0, TOKENS, WIDE):
        tokens = slice(token, token + WIDE)
        rows = jnp.concatenate([pair[tokens, :] for pair in next_pairs], axis=1)
        store_output(output_ref, token, turned_product(weights, rows))


def turn_kernel(parts_ref, out_ref):
    turned = parts_ref[...].reshape(SIDE * COLS, LANES).T
    out_ref[...] = turned.reshape(REPLICAS, LANES // REPLICAS, SIDE * COLS)


def gram_kernel(updates_ref, out_ref):
    updates = [updates_ref[r] for r in range(REPLICAS)]
    lines = []
    for i, j in PAIRS:
        product = updates[i] * updates[j]
        lines.append(jnp.sum(product, axis=0, keepdims=True))
    while len(lines) % 8:
        lines.append(jnp.zeros_like(lines[0]))
    sums = jnp.sum(jnp.concatenate(lines, axis=0), axis=1, keepdims=True)
    spread = jnp.broadcast_to(sums, (len(lines), LANES))
    line = lax.broadcasted_iota(jnp.int32, spread.shape, 0)
    lane = lax.broadcasted_iota(jnp.int32, spread.shape, 1)
    packed = jnp.sum(jnp.where(line == lane, spread, 0.0), axis=0, keepdims=True)
    for j in range(REPLICAS):
        out_ref[j] = packed


def gram_sum_kernel(parts_ref, out_ref):
    packed = jnp.sum(parts_ref[...], axis=0)
    for j in range(SIDE * SIDE):
        out_ref[j] = packed


def merge_kernel(parts_ref, updates_ref, out_ref):
    packed = jnp.sum(parts_ref[...], axis=0)
    lane = lax.broadcasted_iota(jnp.int32, packed.shape, 1)
    gram = {}
    for place, (i, j) in enumerate(PAIRS):
        value = jnp.sum(jnp.where(lane == place, packed, 0.0), axis=1, keepdims=True)
        gram[i, j] = value
        gram[j, i] = value
    members = [[r] for r in range(REPLICAS)]
    while len(members) > 1:
        merged = []
        for lower, upper in zip(members[0::2], members[1::2]):
            cross_dot = sum(gram[i, j] for i in lower for j in upper)
            lower_norm = sum(gram[i, j] for i in lower for j in lower)
            upper_norm = sum(gram[i, j] for i in upper for j in upper)
            lower_coef = 1.0 - cross_dot / (2.0 * (lower_norm + norm_eps))
            upper_coef = 1.0 - cross_dot / (2.0 * (upper_norm + norm_eps))
            scale = {**{i: lower_coef for i in lower}, **{i: upper_coef for i in upper}}
            merged.append((lower + upper, scale))
        factor = {i: scale[i] for _, scale in merged for i in scale}
        gram = {(i, j): factor[i] * factor[j] * value for (i, j), value in gram.items()}
        total = factor if len(merged) * 2 == REPLICAS else {i: total[i] * factor[i] for i in total}
        members = [group for group, _ in merged]
    result = total[0] * updates_ref[0]
    for r in range(1, REPLICAS):
        result = result + total[r] * updates_ref[r]
    out_ref[...] = result


def on_device(
    weight,
    first_moment,
    second_moment,
    token_ids,
    shared_inputs,
    private_inputs,
    shared_targets,
    private_targets,
):
    core = lax.axis_index("core")
    z = lax.axis_index("z")
    y = lax.axis_index("y")
    sum_place = jnp.where(core == 0, z, y)
    gather_place = jnp.where(core == 0, y, z)

    own = widened(shared_inputs, private_inputs[0])
    places = jnp.stack([sum_place, gather_place]).astype(jnp.int32)
    ids = token_ids[0].astype(F32).T
    targets = own_targets(places, ids, shared_targets, private_targets[0])

    pairs = []
    upward = downward = held = own
    for hop in range(3):
        if hop >= 2:
            upward, pairs[hop - 2] = lax.optimization_barrier((upward, pairs[hop - 2]))
        upward = lax.ppermute(upward, CZY, UP)
        downward = lax.ppermute(downward, CZY, DOWN)
        steps = range(STEPS // 2 if hop == 1 else STEPS)
        pairs.append(chosen_rows(ids, held, upward, tuple(steps)))
        if hop == 1:
            second = (held, upward)
        held = downward
    upward, pairs[1] = lax.optimization_barrier((upward, pairs[1]))
    opposite = lax.ppermute(upward, CZY, UP)
    rest = chosen_rows(ids, *second, tuple(range(STEPS // 2, STEPS)))
    pairs[2], rest = lax.optimization_barrier((pairs[2], rest))
    pairs[1] = [*pairs[1], *rest]

    start = kernel_call(
        states_kernel, shaped(SIDE, 3 * COLS, LANES), weight, first_moment[0], second_moment[0]
    )
    start = exchange(start, CZY, GATHER_GROUPS)
    start, part = kernel_call(
        early_kernel,
        [shaped(SIDE, 3 * COLS, LANES), shaped(COLS, TOKENS)],
        places,
        start,
        targets,
        *[pair[0] for pair in pairs],
    )
    *late, parts = kernel_call(
        late_kernel,
        [shaped(TOKENS, WIDE, dtype=BF16)] * STEPS + [shaped(SIDE, COLS, LANES)],
        ids,
        start,
        held,
        opposite,
        part,
    )
    pairs.append(late)
    states = start
    for step in range(STEPS):
        parts = exchange(parts, CZY, SUM_GROUPS)
        error = kernel_call(
            functools.partial(error_kernel, step), shaped(SIDE, COLS, LANES), parts, targets
        )
        error = exchange(error, CZY, SUM_GROUPS)
        last = step == STEPS - 1
        body = functools.partial(step_kernel, step == 0, last)
        operands = (places, error, start, states, *[pair[step] for pair in pairs])
        if last:
            updates = kernel_call(body, shaped(SIDE, COLS, LANES), *operands)
        else:
            states, parts = kernel_call(
                body,
                [shaped(SIDE, 3 * COLS, LANES), shaped(SIDE, COLS, LANES)],
                *operands,
                *[pair[step + 1] for pair in pairs],
            )

    updates = exchange(updates, CZY, GATHER_GROUPS)
    turned = kernel_call(turn_kernel, shaped(REPLICAS, LANES // REPLICAS, SIDE * COLS), updates)
    updates = exchange(turned, ("x", "core"))
    gram = kernel_call(gram_kernel, shaped(REPLICAS, 1, LANES), updates)
    gram = exchange(gram, ("x", "core"))
    gram = kernel_call(gram_sum_kernel, shaped(SIDE * SIDE, 1, LANES), gram)
    gram = exchange(gram, ("z", "y"))
    return kernel_call(
        merge_kernel, shaped(LANES // REPLICAS, SIDE * COLS), gram, updates
    )


def solution(mesh):
    torus = Mesh(mesh.devices.reshape(4, 2, SIDE, SIDE), ("x", "core", "z", "y"))
    row = ("z", "y")
    rep = ("x", "core")
    placed = (
        P(row, None),
        P(rep, row, None),
        P(rep, row, None),
        P(rep, None, None),
        P(None, row),
        P(rep, None, row),
        P(),
        P(rep, None, None),
    )
    return jax.shard_map(
        on_device,
        mesh=torus,
        in_specs=placed,
        out_specs=P((*row, *rep), None),
        check_vma=False,
    )
```
